32 devices in a mesh: grp: 2 (over y), space: 4 (over z), mem: 4 (over x, core).
Axes of the slice: x: 2, y: 2, z: 4, core: 2. Of those that a mesh axis runs over, the one named last changes fastest.
Arguments:
- starting_states: bfloat16 [8, 100, 4096], P(('grp', 'mem'), None, 'space'), parts along dimension 0, may hold values from -12 to 12
- observed: bfloat16 [200, 4096], P('grp', 'space'), parts along dimension 0, may hold values from -12 to 12
- mesh_feat: bfloat16 [512, 512], P('space'), may hold values from -6 to 6
- enc_send: int32 [4, 4, 128], P('space'), may hold values from 0 to 1023
- enc_edges: int32 [512, 16], P('space'), may hold values from 0 to 511, as said below
- dec_send: int32 [4, 4, 32], P('space'), may hold values from 0 to 127
- dec_edges: int32 [4096, 3], P('space'), may hold values from 0 to 127, as said below
- w_in: bfloat16 [100, 512], replicated, may hold values from -0.625 to 0.625
- w_src: bfloat16 [512, 512], replicated, may hold values from -0.25 to 0.25
- w_dst: bfloat16 [512, 512], replicated, may hold values from -0.25 to 0.25
- w_enc: bfloat16 [512, 512], replicated, may hold values from -0.25 to 0.25
- w_msg: bfloat16 [512, 512], replicated, may hold values from -0.25 to 0.25
- w_self: bfloat16 [512, 512], replicated, may hold values from -0.25 to 0.25
- w_hid: bfloat16 [512, 512], replicated, may hold values from -0.25 to 0.25
- decoder_variable_matrix: bfloat16 [512, 100], replicated, may hold values from -0.25 to 0.25
Outputs:
- predicted_member_states: bfloat16 [8, 100, 4096], P(('grp', 'mem'), None, 'space'), parts along dimension 0
- energy_loss: float32 [2], P('grp'), parts along dimension 0
- grad_out: float32 [1024, 100], P('grp'), parts along dimension 0
- grad_msg: bfloat16 [1024, 512], P('grp'), parts along dimension 0
The draws below stay inside these ranges and needn't reach their ends.
There are 2 independent parts, one for each index of `grp`. The reference program is written for one: setup_inputs(seed, part) draws one part's arguments, and reference() takes and returns one part's arrays. A program takes and returns all parts, laid end to end along the dimension named above; an argument that names none is the same for every part. Nothing has to cross between parts.
Inputs may be any that keep to these rules, and one draw needn't show every extreme that they name: `enc_send`: entry [s, d, t] is the row of the grid points of index s that fills slot t of what s sends to d; a slot may repeat a row. `dec_send`: entry [s, d, t] is the row of the mesh nodes of index s that fills slot t of what s sends to d; a slot may repeat a row. `enc_edges`: for the nodes held by index d of space, each entry is s * 128 + t for a slot t among the first slots that source s fills for d; every filled slot is named by some entry of d; each of the 1 sources with a refined region fills all 128 slots to every d, the last index of space fills all of them to index 0, the other pairs fewer. `dec_edges`: for the grid points held by index d of space, each entry is s * 32 + t for a slot t among the first slots that source s fills for d; every filled slot is named by some entry of d; each of the 1 indices with a refined region receives all 32 slots from every source, index 0 receives all of them from the last index of space, the other pairs fewer.
All inputs are finite; a program needn't handle non-finite values.
Results may differ from the reference program's by a relative error of at most 0.007.
Values may be sent and summed in bfloat16 or wider, within the bound.
A program may use at most 128 MiB of HBM per device.

```python
import math
import jax
import jax.numpy as jnp
from jax import lax

VARS = 100
LATENT = 512
K_ENC = 16
K_DEC = 3
G_DEV = 1024
N_DEV = 128
REFINED = 1
E_CAP = 128
D_CAP = 32
GRID = 4096
NODES = 512
MEMBERS = 4
N_SPACE = 4


def field_common(key):
    scale_key = jax.random.fold_in(key, 101)
    shape_key = jax.random.fold_in(key, 102)
    cell_key = jax.random.fold_in(key, 103)
    spread = jnp.exp(jax.random.uniform(scale_key, (VARS, 1), jnp.float32, -0.8, 0.8))
    ramp = 0.6 + 1.2 * jnp.arange(GRID, dtype=jnp.float32)[None, :] / GRID
    roughness = jax.random.uniform(cell_key, (1, GRID), jnp.float32, 0.6, 1.6)
    envelope = spread * ramp * roughness
    common = jax.random.normal(shape_key, (VARS, GRID), jnp.float32) * envelope
    return (common, envelope)


def refined_owners(key):
    owner_key = jax.random.fold_in(key, 201)
    scores = jax.random.randint(owner_key, (N_SPACE,), 0, 1 << 20) * N_SPACE + jnp.arange(N_SPACE, dtype=jnp.int32)
    ranking = jnp.argsort(jnp.argsort(scores))
    return ranking < REFINED


def slot_edges(key, capacity, row_count, fanout, full_pairs):
    count_key = jax.random.fold_in(key, 1)
    pick_key = jax.random.fold_in(key, 2)
    shuffle_key = jax.random.fold_in(key, 3)
    lowest = max(1, capacity // 8)
    highest = max(lowest + 1, capacity // 2 + 1)
    indices = jnp.arange(N_SPACE, dtype=jnp.int32)
    last_pair = (indices[:, None] == N_SPACE - 1) & (indices[None, :] == 0)
    counts = jnp.where(full_pairs | last_pair, capacity, jax.random.randint(count_key, (N_SPACE, N_SPACE), lowest, highest))
    per_target = jnp.transpose(counts)
    block_ends = jnp.cumsum(per_target, axis=1)
    live_total = block_ends[:, -1:]
    edge_total = row_count * fanout
    position = jnp.arange(edge_total, dtype=jnp.int32)[None, :]
    random_rank = jax.random.randint(pick_key, (N_SPACE, edge_total), 0, live_total)
    live_rank = jnp.where(position < live_total, position, random_rank)
    source = jnp.sum((live_rank[:, :, None] >= block_ends[:, None, :]).astype(jnp.int32), axis=2)
    block_starts = block_ends - per_target
    offset = live_rank - jnp.take_along_axis(block_starts, source, axis=1)
    slot_value = source * capacity + offset
    score_top = (1 << 30) // edge_total
    scores = jax.random.randint(shuffle_key, (N_SPACE, edge_total), 0, score_top) * edge_total + position
    shuffle = jnp.argsort(scores, axis=1)
    slot_value = jnp.take_along_axis(slot_value, shuffle, axis=1)
    return slot_value.reshape(N_SPACE * row_count, fanout).astype(jnp.int32)


def draw_starting_states(key, part):
    common, envelope = field_common(key)
    key = jax.random.fold_in(key, 7)
    noise = jax.random.normal(key, (MEMBERS, VARS, GRID), jnp.float32)
    values = common[None] + 0.6 * noise * envelope[None]
    return jnp.clip(values, -12.0, 12.0).astype(jnp.bfloat16)


def draw_observed(key, part):
    common, envelope = field_common(key)
    key = jax.random.fold_in(key, 8)
    noise = jax.random.normal(key, (VARS, GRID), jnp.float32)
    values = common + 0.5 * noise * envelope
    return jnp.clip(values, -12.0, 12.0).astype(jnp.bfloat16)


def draw_enc_edges(key, part):
    refined = refined_owners(key)
    key = jax.random.fold_in(key, 11)
    full_pairs = jnp.broadcast_to(refined[:, None], (N_SPACE, N_SPACE))
    return slot_edges(key, E_CAP, N_DEV, K_ENC, full_pairs)


def draw_dec_edges(key, part):
    refined = refined_owners(key)
    key = jax.random.fold_in(key, 12)
    full_pairs = jnp.broadcast_to(refined[None, :], (N_SPACE, N_SPACE))
    return slot_edges(key, D_CAP, G_DEV, K_DEC, full_pairs)


def plant(drawn, rng, least, largest):
    index_at = [jax.random.randint(jax.random.fold_in(rng, axis), (), 0, length) for axis, length in enumerate(drawn.shape)]
    main_axis = drawn.shape.index(max(drawn.shape))
    neighbour = index_at[:main_axis] + [(index_at[main_axis] + 1) % drawn.shape[main_axis]] + index_at[main_axis + 1:]
    return drawn.at[tuple(index_at)].set(least).at[tuple(neighbour)].set(largest)


def block_scale(own_key, extent, split, low, high):
    gain, own = 1.0, jax.random.fold_in(own_key, 6)
    for dim, parts in split:
        draws = jnp.exp(jax.random.uniform(jax.random.fold_in(own, dim), (parts,), jnp.float32, low / len(split), high / len(split)))
        gain = gain * jnp.repeat(draws, extent[dim] // parts).reshape([-1 if axis == dim else 1 for axis in range(len(extent))])
    return gain


def normal_values(rng, extent, width, reach, shards=(), held_as=jnp.bfloat16):
    factor_of = block_scale(rng, extent, shards, -0.22, 0.18) if shards else 1.0
    values = jax.random.normal(rng, extent, jnp.float32) * width * factor_of
    return jnp.minimum(jnp.maximum(values, -reach), reach).astype(held_as)


def setup_inputs(seed: int = 0, part: int = 0) -> dict:
    splits = jax.random.split(jax.random.key(seed), 16)
    own_keys = jax.random.split(jax.random.fold_in(splits[15], part), 16)
    return {
        "starting_states": draw_starting_states(jax.random.fold_in(jax.random.fold_in(splits[15], part), 71), part),
        "observed": draw_observed(jax.random.fold_in(jax.random.fold_in(splits[15], part), 71), part),
        "mesh_feat": normal_values(splits[2], (NODES, LATENT), 1.0, 6.0, ((0, 4),)),
        "enc_send": plant(jax.random.randint(splits[3], (N_SPACE, N_SPACE, E_CAP), 0, G_DEV), jax.random.fold_in(splits[3], 1), 0, G_DEV - 1).astype(jnp.int32),
        "enc_edges": draw_enc_edges(jax.random.fold_in(splits[15], 71), part),
        "dec_send": plant(jax.random.randint(splits[5], (N_SPACE, N_SPACE, D_CAP), 0, N_DEV), jax.random.fold_in(splits[5], 1), 0, N_DEV - 1).astype(jnp.int32),
        "dec_edges": draw_dec_edges(jax.random.fold_in(splits[15], 71), part),
        "w_in": normal_values(splits[7], (VARS, LATENT), VARS ** -0.5, 0.625),
        "w_src": normal_values(splits[8], (LATENT, LATENT), LATENT ** -0.5, 0.25),
        "w_dst": normal_values(splits[9], (LATENT, LATENT), LATENT ** -0.5, 0.25),
        "w_enc": normal_values(splits[10], (LATENT, LATENT), LATENT ** -0.5, 0.25),
        "w_msg": normal_values(splits[11], (LATENT, LATENT), LATENT ** -0.5, 0.25),
        "w_self": normal_values(splits[12], (LATENT, LATENT), LATENT ** -0.5, 0.25),
        "w_hid": normal_values(splits[13], (LATENT, LATENT), LATENT ** -0.5, 0.25),
        "decoder_variable_matrix": normal_values(splits[14], (LATENT, VARS), LATENT ** -0.5, 0.25),
    }


def silu_slope(argument):
    logistic = jax.nn.sigmoid(argument)
    return logistic * (1.0 + argument * (1.0 - logistic))

def grid_pass(members_state_array, mesh_feat, enc_send, enc_edges, dec_send, dec_edges, w_in, w_src, w_dst, w_enc, w_msg, w_self, w_hid):
    grid_latent = jax.nn.silu(jnp.einsum('vg,vh->gh', members_state_array.astype(jnp.float32), w_in.astype(jnp.float32))).astype(jnp.bfloat16)
    projected = jnp.dot(grid_latent, w_src, preferred_element_type=jnp.float32).astype(jnp.bfloat16)
    sources = jnp.arange(N_SPACE, dtype=jnp.int32)[:, None, None]
    enc_index = jnp.transpose(enc_send + sources * G_DEV, (1, 0, 2)).reshape(-1)
    arrivals = jnp.take(projected, enc_index, axis=0)
    node_owner = (jnp.arange(NODES, dtype=jnp.int32) // N_DEV)[:, None]
    neighbours = jnp.take(arrivals, enc_edges + node_owner * (N_SPACE * E_CAP), axis=0).astype(jnp.float32)
    node_query = jnp.dot(mesh_feat, w_dst, preferred_element_type=jnp.float32).astype(jnp.bfloat16)
    aggregate = lax.optimization_barrier(jnp.mean(jax.nn.silu(neighbours + node_query.astype(jnp.float32)[:, None, :]), axis=1)).astype(jnp.bfloat16)
    mesh_latent = (mesh_feat.astype(jnp.float32) + jnp.dot(aggregate, w_enc, preferred_element_type=jnp.float32)).astype(jnp.bfloat16)
    dec_index = jnp.transpose(dec_send + sources * N_DEV, (1, 0, 2)).reshape(-1)
    mesh_arrivals = jnp.take(mesh_latent, dec_index, axis=0)
    message = jnp.dot(mesh_arrivals, w_msg, preferred_element_type=jnp.float32).astype(jnp.bfloat16)
    grid_owner = (jnp.arange(GRID, dtype=jnp.int32) // G_DEV)[:, None]
    slot_index = dec_edges + grid_owner * (N_SPACE * D_CAP)
    self_term = jnp.dot(grid_latent, w_self, preferred_element_type=jnp.float32)
    decoder_in = jnp.take(message, slot_index, axis=0).astype(jnp.float32) + self_term[:, None, :]
    updated = (grid_latent.astype(jnp.float32) + lax.optimization_barrier(jnp.mean(jax.nn.silu(decoder_in), axis=1))).astype(jnp.bfloat16)
    hidden_pre = jnp.dot(updated, w_hid, preferred_element_type=jnp.float32)
    return (mesh_arrivals, slot_index, decoder_in, updated, hidden_pre)

def reference(starting_states, observed, mesh_feat, enc_send, enc_edges, dec_send, dec_edges, w_in, w_src, w_dst, w_enc, w_msg, w_self, w_hid, decoder_variable_matrix):
    weights_in = (mesh_feat, enc_send, enc_edges, dec_send, dec_edges, w_in, w_src, w_dst, w_enc, w_msg, w_self, w_hid)

    def predicted_state_numbers(members_state_array):
        unused_a, unused_b, unused_c, unused_d, hidden_pre = grid_pass(members_state_array, *weights_in)
        inner_layer_response = jax.nn.silu(hidden_pre).astype(jnp.bfloat16)
        increment = jnp.einsum('gh,hv->vg', inner_layer_response.astype(jnp.float32), decoder_variable_matrix.astype(jnp.float32))
        return (members_state_array.astype(jnp.float32) + increment).astype(jnp.bfloat16)
    predicted_member_states = lax.map(predicted_state_numbers, starting_states)
    observed_f = observed.astype(jnp.float32)
    entries = VARS * GRID
    member_total_number = MEMBERS
    scale_factor = member_total_number * math.sqrt(entries)

    def square_sums(member):
        member_f = member.astype(jnp.float32)
        diff = member_f - observed_f
        apart = predicted_member_states.astype(jnp.float32) - member_f[None]
        return (jnp.sum(diff * diff), lax.optimization_barrier(jnp.sum(apart * apart, axis=(1, 2))))
    error_sq, pair_sq = lax.map(square_sums, predicted_member_states)
    errors = jnp.sqrt(error_sq / entries + 1e-06)
    spreads = jnp.sqrt(pair_sq / entries + 1e-06)
    apart_mask = 1.0 - jnp.eye(member_total_number, dtype=jnp.float32)
    energy_loss = jnp.mean(errors) - jnp.sum(apart_mask * spreads) / (2.0 * member_total_number * member_total_number)
    weights = apart_mask / (member_total_number * member_total_number * entries * spreads)

    def members_state_derivative(member_index):
        member = predicted_member_states[member_index].astype(jnp.float32)
        first = (member - observed_f) / (member_total_number * entries * errors[member_index])
        pulled = jnp.einsum('b,bvg->vg', weights[member_index], member[None] - predicted_member_states.astype(jnp.float32))
        return (scale_factor * (first - pulled)).astype(jnp.bfloat16)
    predicted_state_derivative = lax.map(members_state_derivative, jnp.arange(member_total_number, dtype=jnp.int32))

    def backward_derivative_pass(pair):
        members_state_array, member_grad = pair
        mesh_arrivals, slot_index, decoder_in, updated, hidden_pre = grid_pass(members_state_array, *weights_in)
        inner_layer_response = jax.nn.silu(hidden_pre).astype(jnp.bfloat16)
        part_out = jnp.einsum('fu,sf->us', inner_layer_response.astype(jnp.float32), member_grad.astype(jnp.float32))
        hidden_gradient = jnp.einsum('tm,lt->ml', member_grad.astype(jnp.float32), decoder_variable_matrix.astype(jnp.float32))
        pre_grad = (hidden_gradient * silu_slope(hidden_pre)).astype(jnp.bfloat16)
        updated_grad = jnp.einsum('gk,hk->gh', pre_grad.astype(jnp.float32), w_hid.astype(jnp.float32))
        edge_grad = updated_grad[:, None, :] * silu_slope(decoder_in) / K_DEC
        message_grad = jax.ops.segment_sum(edge_grad.reshape(-1, LATENT), slot_index.reshape(-1), num_segments=N_SPACE * N_SPACE * D_CAP).astype(jnp.bfloat16)
        part_msg = jnp.einsum('rh,rk->hk', mesh_arrivals.astype(jnp.float32), message_grad.astype(jnp.float32))
        return (part_out, part_msg)
    incomplete_decoder_result, incomplete_edge_signal = lax.map(backward_derivative_pass, (starting_states, predicted_state_derivative))
    return (predicted_member_states, jnp.reshape(energy_loss, (1,)), lax.optimization_barrier(jnp.sum(incomplete_decoder_result, axis=0)), lax.optimization_barrier(jnp.sum(incomplete_edge_signal, axis=0)).astype(jnp.bfloat16))
```

```python
import functools
import math

import jax
import jax.numpy as jnp
from jax import lax
from jax.experimental import pallas as pl
from jax.experimental.pallas import tpu as pltpu
from jax.sharding import PartitionSpec as P

MESH = pl.DeviceIdType.MESH
F32 = jnp.float32
BF16 = jnp.bfloat16
ROWS = 112
CHUNKS = 4


def dot(a, b, contract=(1, 0)):
    return lax.dot_general(
        a, b, (((contract[0],), (contract[1],)), ((), ())), preferred_element_type=F32
    )


def sigmoid(v):
    return 0.5 * jnp.tanh(0.5 * v) + 0.5


def silu(v):
    return v * sigmoid(v)


def slope(v):
    g = sigmoid(v)
    return g * (1.0 + v * (1.0 - g))


def one_hot(hit):
    return jnp.where(hit, 1.0, 0.0).astype(BF16)


def step_kernel(
    spaces, members,
    x_ref, obs_ref, feat_ref, esend_ref, eedge_ref, dsend_ref, dedge_ref, dedge_t_ref,
    w_in_ref, w_src_ref, w_dst_ref, w_enc_ref, w_msg_ref, w_self_ref, w_hid_ref, dvm_t_ref,
    pred_ref, loss_ref, gout_ref, gmsg_ref,
    xp, obsp, winp, dvmp,
    xs_send, xs_recv, gl, self_term, ehot, dhot, dhot_t, arr_gl, arr, nq,
    ms_send, ma, dec_in, hid, act, ens, st, st_recv, loss_s, loss_r, fgs,
    gos, gor, gs, gq, aall, at, q32, qb, q_recv, gq32, gq_recv, fin, gfin,
    x_ss, x_rs, m_ss, m_rs, e_ss, e_rs, a_ss, a_rs, s_ss, s_rs, l_ss, l_rs,
    o_ss, o_rs, g_ss, g_rs, zq_ss, zq_rs, zo_ss, zo_rs, c1_ss, c1_rs, d1_ss, d1_rs,
    c2_ss, c2_rs, d2_ss, d2_rs,
):
    grp, sp, me = lax.axis_index("grp"), lax.axis_index("space"), lax.axis_index("mem")
    varn, grid = obs_ref.shape
    latent = w_src_ref.shape[0]
    nodes = feat_ref.shape[0]
    ecap, dcap = esend_ref.shape[2], dsend_ref.shape[2]
    slots, dslots = spaces * ecap, spaces * dcap
    k_enc, k_dec = eedge_ref.shape[1], dedge_ref.shape[1]
    part = grid // CHUNKS
    entries = varn * grid * spaces
    quarter = latent // members
    zrows = latent // spaces

    def space_at(o):
        return lax.rem(sp + o, spaces)

    def mem_at(o):
        return lax.rem(me + o, members)

    def to_space(src, dst, ss, rs, o):
        return pltpu.make_async_remote_copy(
            src_ref=src, dst_ref=dst, send_sem=ss.at[o], recv_sem=rs.at[o],
            device_id=(grp, space_at(o), me), device_id_type=MESH,
        )

    def to_mem(src, dst, ss, rs, o):
        return pltpu.make_async_remote_copy(
            src_ref=src, dst_ref=dst, send_sem=ss, recv_sem=rs,
            device_id=(grp, sp, mem_at(o)), device_id_type=MESH,
        )

    barrier = pltpu.get_barrier_semaphore()
    for o in range(1, spaces):
        pl.semaphore_signal(barrier, inc=1, device_id=(grp, space_at(o), me), device_id_type=MESH)
    for o in range(1, members):
        pl.semaphore_signal(barrier, inc=1, device_id=(grp, sp, mem_at(o)), device_id_type=MESH)

    xp[96:ROWS, :] = jnp.zeros((ROWS - 96, grid), BF16)
    xp[0:varn, :] = x_ref[0]
    winp[96:ROWS, :] = jnp.zeros((ROWS - 96, latent), BF16)
    winp[0:varn, :] = w_in_ref[...]

    grid_rows = lax.broadcasted_iota(jnp.int32, (grid, ecap), 0)
    xs = []
    waited = False
    for o in list(range(1, spaces)) + [0]:
        row = esend_ref[0, pl.ds(space_at(o), 1), :]
        hot = one_hot(grid_rows == row)
        picked = dot(xp[...], hot).astype(BF16)
        if o == 0:
            xs_recv[sp] = picked
        else:
            xs_send[o] = picked
            if not waited:
                pl.semaphore_wait(barrier, spaces + members - 2)
                waited = True
            copy = to_space(xs_send.at[o], xs_recv.at[sp], x_ss, x_rs, o)
            copy.start()
            xs.append(copy)

    obsp[96:ROWS, :] = jnp.zeros((ROWS - 96, grid), BF16)
    obsp[0:varn, :] = obs_ref[...]
    dvmp[96:ROWS, :] = jnp.zeros((ROWS - 96, latent), BF16)
    dvmp[0:varn, :] = dvm_t_ref[...]
    nq[...] = dot(feat_ref[...], w_dst_ref[...]).astype(BF16).astype(F32)
    slot_cols = lax.broadcasted_iota(jnp.int32, (nodes, slots), 1)
    for k in range(k_enc):
        ehot[k * nodes:(k + 1) * nodes, :] = one_hot(slot_cols == eedge_ref[:, k:k + 1])
    for c in range(CHUNKS):
        rows = slice(c * part, (c + 1) * part)
        gl[rows, :] = silu(dot(xp[:, rows], winp[...], (0, 0))).astype(BF16)

    for copy in xs:
        copy.wait()
    for s in range(spaces):
        arr_gl[s * ecap:(s + 1) * ecap, :] = silu(dot(xs_recv[s], winp[...], (0, 0))).astype(BF16)
    arr[...] = dot(arr_gl[...], w_src_ref[...]).astype(BF16)
    total = jnp.zeros((nodes, latent), F32)
    group = 4
    for k in range(0, k_enc, group):
        v = dot(ehot[k * nodes:(k + group) * nodes, :], arr[...])
        for i in range(group):
            total += silu(v[i * nodes:(i + 1) * nodes, :] + nq[...])
    aggregate = (total * (1.0 / k_enc)).astype(BF16)
    mesh_latent = (feat_ref[...].astype(F32) + dot(aggregate, w_enc_ref[...])).astype(BF16)

    node_rows = lax.broadcasted_iota(jnp.int32, (nodes, dcap), 0)
    ms = []
    for o in list(range(1, spaces)) + [0]:
        row = dsend_ref[0, pl.ds(space_at(o), 1), :]
        picked = dot(one_hot(node_rows == row), mesh_latent, (0, 0)).astype(BF16)
        if o == 0:
            ma[sp] = picked
        else:
            ms_send[o] = picked
            copy = to_space(ms_send.at[o], ma.at[sp], m_ss, m_rs, o)
            copy.start()
            ms.append(copy)
    dcols = lax.broadcasted_iota(jnp.int32, (grid, dslots), 1)
    drows = lax.broadcasted_iota(jnp.int32, (dslots, grid), 0)
    for k in range(k_dec):
        dhot[k] = one_hot(dcols == dedge_ref[:, k:k + 1])
        dhot_t[k] = one_hot(drows == dedge_t_ref[k:k + 1, :])
    for c in range(CHUNKS):
        rows = slice(c * part, (c + 1) * part)
        self_term[rows, :] = dot(gl[rows, :], w_self_ref[...])
    for copy in ms:
        copy.wait()

    arrivals = ma[...].reshape(dslots, latent)
    aall[0] = arrivals
    message = dot(arrivals, w_msg_ref[...]).astype(BF16)
    es = []
    for c in range(CHUNKS):
        rows = slice(c * part, (c + 1) * part)
        acc = jnp.zeros((part, latent), F32)
        own = self_term[rows, :]
        for k in range(k_dec):
            v = dot(dhot[k, rows, :], message) + own
            dec_in[k, rows, :] = v
            acc += silu(v)
        updated = (gl[rows, :].astype(F32) + acc * (1.0 / k_dec)).astype(BF16)
        pre = dot(updated, w_hid_ref[...])
        hid[rows, :] = pre
        response = silu(pre).astype(BF16)
        act[rows, :] = response
        increment = dot(dvmp[...], response, (1, 1))
        predicted = (xp[:, rows].astype(F32) + increment).astype(BF16)
        ens[0, c] = predicted
        pred_ref[0, :, rows] = predicted[0:varn, :]
        for o in range(1, members):
            copy = to_mem(
                ens.at[0, c], ens.at[members - o, c], e_ss.at[o, c], e_rs.at[o, c], o
            )
            copy.start()
            es.append(copy)
    as_ = []
    for o in range(1, members):
        copy = to_mem(aall.at[0], aall.at[members - o], a_ss.at[o], a_rs.at[o], o)
        copy.start()
        as_.append(copy)

    for c in range(CHUNKS):
        rows = slice(c * part, (c + 1) * part)
        hid[rows, :] = slope(hid[rows, :])
        for k in range(k_dec):
            dec_in[k, rows, :] = slope(dec_in[k, rows, :]) * (1.0 / k_dec)

    def folded(d):
        d = (d * d).reshape(ROWS // 8, 8, part).sum(axis=0)
        out = d[:, 0:128]
        for i in range(1, part // 128):
            out += d[:, i * 128:(i + 1) * 128]
        return out

    sums = [jnp.zeros((8, 128), F32) for _ in range(members)]
    for copy in es:
        copy.wait()
    for c in range(CHUNKS):
        rows = slice(c * part, (c + 1) * part)
        mine = ens[0, c].astype(F32)
        sums[0] += folded(mine - obsp[:, rows].astype(F32))
        for j in range(1, members):
            sums[j] += folded(mine - ens[j, c].astype(F32))
    for j in range(members):
        st[j] = sums[j]
    ss = []
    for o in range(1, spaces):
        copy = to_space(st, st_recv.at[o], s_ss, s_rs, o)
        copy.start()
        ss.append(copy)
    for copy in ss:
        copy.wait()
    tot = st[...]
    for o in range(1, spaces):
        tot += st_recv[o]
    root = jnp.sqrt(jnp.sum(tot, axis=(1, 2), keepdims=True) / entries + 1e-06)
    error = root[0]
    my_loss = error / members
    for j in range(1, members):
        my_loss -= root[j] / (2.0 * members * members)
    loss_s[...] = jnp.broadcast_to(my_loss, (8, 128))
    ls = []
    for o in range(1, members):
        copy = to_mem(loss_s, loss_r.at[o], l_ss.at[o], l_rs.at[o], o)
        copy.start()
        ls.append(copy)
    scale = members * math.sqrt(entries)
    first = scale / (members * entries * error)
    pulls = [scale / (members * members * entries * root[j]) for j in range(1, members)]

    gout = jnp.zeros((ROWS, latent), F32)
    for c in range(CHUNKS):
        rows = slice(c * part, (c + 1) * part)
        mine = ens[0, c].astype(F32)
        fg = first * (mine - obsp[:, rows].astype(F32))
        for j in range(1, members):
            fg -= pulls[j - 1] * (mine - ens[j, c].astype(F32))
        fg = fg.astype(BF16)
        fgs[c] = fg
        gout += dot(fg, act[rows, :])
    for m in range(members):
        gos[m, 0:ROWS, :] = gout[:, m * quarter:(m + 1) * quarter]
        gos[m, ROWS:128, :] = jnp.zeros((128 - ROWS, quarter), F32)
    os_ = []
    for o in range(1, members):
        copy = to_mem(gos.at[mem_at(o)], gor.at[o], o_ss.at[o], o_rs.at[o], o)
        copy.start()
        os_.append(copy)

    mgrad = jnp.zeros((dslots, latent), F32)
    for c in range(CHUNKS):
        rows = slice(c * part, (c + 1) * part)
        hgrad = dot(fgs[c], dvmp[...], (0, 0))
        pre_grad = (hgrad * hid[rows, :]).astype(BF16)
        ugrad = dot(pre_grad, w_hid_ref[...], (1, 1))
        for k in range(k_dec):
            edge = (ugrad * dec_in[k, rows, :]).astype(BF16)
            mgrad += dot(dhot_t[k, :, rows], edge)
    for m in range(members):
        gs[m] = mgrad[:, m * quarter:(m + 1) * quarter].astype(BF16)
    gsent = []
    for o in range(1, members):
        copy = to_mem(gs.at[mem_at(o)], gq.at[members - o], g_ss.at[o], g_rs.at[o], o)
        copy.start()
        gsent.append(copy)
    gq[0] = gs[me]
    for copy in as_:
        copy.wait()
    for j in range(members):
        at[:, j * dslots:(j + 1) * dslots] = aall[j].astype(F32).T.astype(BF16)
    for copy in os_:
        copy.wait()
    oq = gos[me]
    for o in range(1, members):
        oq += gor[o]
    gq32[...] = oq.reshape(spaces, 128 // spaces, quarter)
    zo = []
    for o in range(1, spaces):
        copy = to_space(gq32.at[space_at(o)], gq_recv.at[o], zo_ss, zo_rs, o)
        copy.start()
        zo.append(copy)
    for copy in gsent:
        copy.wait()
    q = dot(at[...], gq[...].reshape(members * dslots, quarter)).reshape(spaces, zrows, quarter)
    q32[...] = q
    qb[...] = q.astype(BF16)
    zq = []
    for o in range(1, spaces):
        copy = to_space(qb.at[space_at(o)], q_recv.at[o], zq_ss, zq_rs, o)
        copy.start()
        zq.append(copy)
    for copy in zo:
        copy.wait()
    gsum = gq32[sp]
    for o in range(1, spaces):
        gsum += gq_recv[o]
    gfin[me, sp] = gsum
    d1 = []
    for o in range(1, spaces):
        copy = to_space(gfin.at[me, sp], gfin.at[me, sp], d1_ss, d1_rs, o)
        copy.start()
        d1.append(copy)
    for copy in zq:
        copy.wait()
    r = q32[sp]
    for o in range(1, spaces):
        r += q_recv[o].astype(F32)
    fin[me, sp] = r.astype(BF16)
    c1 = []
    for o in range(1, spaces):
        copy = to_space(fin.at[me, sp], fin.at[me, sp], c1_ss, c1_rs, o)
        copy.start()
        c1.append(copy)
    for copy in d1:
        copy.wait()
    d2 = []
    for o in range(1, members):
        copy = to_mem(gfin.at[me], gfin.at[me], d2_ss.at[o], d2_rs.at[o], o)
        copy.start()
        d2.append(copy)
    for copy in c1:
        copy.wait()
    c2 = []
    for o in range(1, members):
        copy = to_mem(fin.at[me], fin.at[me], c2_ss.at[o], c2_rs.at[o], o)
        copy.start()
        c2.append(copy)
    for copy in ls:
        copy.wait()
    all_loss = loss_s[...]
    for o in range(1, members):
        all_loss += loss_r[o]
    loss_ref[0] = jnp.max(all_loss)
    for copy in d2:
        copy.wait()
    for m in range(members):
        block = gfin[m].reshape(128, quarter).T
        gout_ref[m * quarter:(m + 1) * quarter, :] = block[:, 0:varn]
    for copy in c2:
        copy.wait()
    for m in range(members):
        gmsg_ref[:, m * quarter:(m + 1) * quarter] = fin[m].reshape(latent, quarter)


def fused(
    starting_states, observed, mesh_feat, enc_send, enc_edges, dec_send, dec_edges,
    w_in, w_src, w_dst, w_enc, w_msg, w_self, w_hid, decoder_variable_matrix,
):
    spaces, members = lax.axis_size("space"), lax.axis_size("mem")
    varn, grid = observed.shape
    latent = w_src.shape[0]
    nodes = mesh_feat.shape[0]
    ecap, dcap = enc_send.shape[2], dec_send.shape[2]
    slots, dslots = spaces * ecap, spaces * dcap
    k_enc, k_dec = enc_edges.shape[1], dec_edges.shape[1]
    part = grid // CHUNKS
    quarter = latent // members
    zrows = latent // spaces
    vmem = pltpu.VMEM
    scratch = [
        vmem((ROWS, grid), BF16), vmem((ROWS, grid), BF16),
        vmem((ROWS, latent), BF16), vmem((ROWS, latent), BF16),
        vmem((spaces, ROWS, ecap), BF16), vmem((spaces, ROWS, ecap), BF16),
        vmem((grid, latent), BF16), vmem((grid, latent), F32),
        vmem((k_enc * nodes, slots), BF16),
        vmem((k_dec, grid, dslots), BF16), vmem((k_dec, dslots, grid), BF16),
        vmem((slots, latent), BF16), vmem((slots, latent), BF16), vmem((nodes, latent), F32),
        vmem((spaces, dcap, latent), BF16), vmem((spaces, dcap, latent), BF16),
        vmem((k_dec, grid, latent), F32), vmem((grid, latent), F32), vmem((grid, latent), BF16),
        vmem((members, CHUNKS, ROWS, part), BF16),
        vmem((members, 8, 128), F32), vmem((spaces, members, 8, 128), F32),
        vmem((8, 128), F32), vmem((members, 8, 128), F32),
        vmem((CHUNKS, ROWS, part), BF16),
        vmem((members, 128, quarter), F32), vmem((members, 128, quarter), F32),
        vmem((members, dslots, quarter), BF16), vmem((members, dslots, quarter), BF16),
        vmem((members, dslots, latent), BF16), vmem((latent, members * dslots), BF16),
        vmem((spaces, zrows, quarter), F32), vmem((spaces, zrows, quarter), BF16),
        vmem((spaces, zrows, quarter), BF16),
        vmem((spaces, 128 // spaces, quarter), F32), vmem((spaces, 128 // spaces, quarter), F32),
        vmem((members, spaces, zrows, quarter), BF16),
        vmem((members, spaces, 128 // spaces, quarter), F32),
    ]
    dma = pltpu.SemaphoreType.DMA
    scratch += [dma((spaces,))] * 4
    scratch += [dma((members, CHUNKS))] * 2
    scratch += [dma((members,))] * 2
    scratch += [dma((spaces,))] * 2
    scratch += [dma((members,))] * 6
    scratch += [dma((spaces,))] * 8
    scratch += [dma((members,))] * 4
    whole = pl.BlockSpec(memory_space=pltpu.VMEM)
    pred, loss, gout, gmsg = pl.pallas_call(
        functools.partial(step_kernel, spaces, members),
        out_shape=(
            jax.ShapeDtypeStruct((1, varn, grid), BF16),
            jax.ShapeDtypeStruct((1,), F32),
            jax.ShapeDtypeStruct((latent, varn), F32),
            jax.ShapeDtypeStruct((latent, latent), BF16),
        ),
        in_specs=[whole] * 16,
        out_specs=(whole, pl.BlockSpec(memory_space=pltpu.SMEM), whole, whole),
        scratch_shapes=scratch,
        compiler_params=pltpu.CompilerParams(
            collective_id=0, has_side_effects=True, vmem_limit_bytes=50 * 1024 * 1024
        ),
    )(
        starting_states, observed, mesh_feat, enc_send, enc_edges, dec_send, dec_edges,
        dec_edges.T, w_in, w_src, w_dst, w_enc, w_msg, w_self, w_hid, decoder_variable_matrix.T,
    )
    return pred, loss, gout, gmsg


def fits(spaces, members, latent, ecap, dcap):
    return (
        latent % (128 * members) == 0
        and latent // members == 128
        and ecap % 128 == 0
        and dcap % 16 == 0
        and latent % (16 * spaces) == 0
        and 128 % (8 * spaces) == 0
    )


def chosen(*args):
    spaces, members = lax.axis_size("space"), lax.axis_size("mem")
    if fits(spaces, members, args[8].shape[0], args[3].shape[2], args[5].shape[2]):
        return fused(*args)
    return local(*args)


def silu_slope(argument):
    logistic = jax.nn.sigmoid(argument)
    return logistic * (1.0 + argument * (1.0 - logistic))


def square_sums(row_block, observed_part):

    def per_member(member):
        member_f = member.astype(jnp.float32)
        diff = member_f - observed_part
        apart = row_block.astype(jnp.float32) - member_f[None]
        return (jnp.sum(diff * diff), jnp.sum(apart * apart, axis=(1, 2)))

    return lax.map(per_member, row_block)


def loss_terms(error_sq, pair_sq, entries):
    member_total_number = error_sq.shape[0]
    errors = jnp.sqrt(error_sq / entries + 1e-06)
    spreads = jnp.sqrt(pair_sq / entries + 1e-06)
    apart_mask = 1.0 - jnp.eye(member_total_number, dtype=jnp.float32)
    energy_loss = jnp.mean(errors) - jnp.sum(apart_mask * spreads) / (
        2.0 * member_total_number * member_total_number
    )
    weights = apart_mask / (member_total_number * member_total_number * entries * spreads)
    return (errors, weights, energy_loss)


def members_state_derivative(
    row_block, member_index, observed_part, errors, weights, scale_factor, entries
):
    member_total_number = row_block.shape[0]
    member = lax.dynamic_index_in_dim(row_block, member_index, 0, keepdims=False).astype(
        jnp.float32
    )
    first = (member - observed_part) / (member_total_number * entries * errors[member_index])

    def add_other(other_member, pulled):
        other_field = lax.dynamic_index_in_dim(row_block, other_member, 0, keepdims=False).astype(
            jnp.float32
        )
        return pulled + weights[member_index, other_member] * (member - other_field)

    pulled = lax.fori_loop(0, member_total_number, add_other, jnp.zeros_like(member))
    return (scale_factor * (first - pulled)).astype(jnp.bfloat16)


def local(
    starting_states,
    observed,
    mesh_feat,
    enc_send,
    enc_edges,
    dec_send,
    dec_edges,
    w_in,
    w_src,
    w_dst,
    w_enc,
    w_msg,
    w_self,
    w_hid,
    decoder_variable_matrix,
):
    members_state_array = starting_states[0]
    spaces = lax.axis_size("space")
    member_total_number = lax.axis_size("mem")
    entries = members_state_array.shape[0] * members_state_array.shape[1] * spaces
    scale_factor = member_total_number * math.sqrt(entries)
    grid_latent = jax.nn.silu(
        jnp.einsum("vg,vh->gh", members_state_array, w_in, preferred_element_type=jnp.float32)
    ).astype(jnp.bfloat16)
    projected = jnp.dot(grid_latent, w_src, preferred_element_type=jnp.float32).astype(jnp.bfloat16)
    outgoing = jnp.take(projected, enc_send[0], axis=0)
    arrived = lax.all_to_all(outgoing, "space", split_axis=0, concat_axis=0, tiled=True)
    received = arrived.reshape(-1, arrived.shape[2])
    node_query = jnp.dot(mesh_feat, w_dst, preferred_element_type=jnp.float32).astype(jnp.bfloat16)
    neighbours = jnp.take(received, enc_edges, axis=0).astype(jnp.float32)
    aggregate = jnp.mean(
        jax.nn.silu(neighbours + node_query.astype(jnp.float32)[:, None, :]), axis=1
    ).astype(jnp.bfloat16)
    mesh_latent = (
        mesh_feat.astype(jnp.float32)
        + jnp.dot(aggregate, w_enc, preferred_element_type=jnp.float32)
    ).astype(jnp.bfloat16)
    outgoing_mesh = jnp.take(mesh_latent, dec_send[0], axis=0)
    arrived_mesh = lax.all_to_all(outgoing_mesh, "space", split_axis=0, concat_axis=0, tiled=True)
    received_mesh = arrived_mesh.reshape(-1, arrived_mesh.shape[2])
    message = jnp.dot(received_mesh, w_msg, preferred_element_type=jnp.float32).astype(jnp.bfloat16)
    self_term = jnp.dot(grid_latent, w_self, preferred_element_type=jnp.float32)
    decoder_in = jnp.take(message, dec_edges, axis=0).astype(jnp.float32) + self_term[:, None, :]
    updated = (grid_latent.astype(jnp.float32) + jnp.mean(jax.nn.silu(decoder_in), axis=1)).astype(
        jnp.bfloat16
    )
    hidden_pre = jnp.dot(updated, w_hid, preferred_element_type=jnp.float32)
    inner_layer_response = jax.nn.silu(hidden_pre).astype(jnp.bfloat16)
    increment = jnp.einsum(
        "gh,hv->vg",
        inner_layer_response,
        decoder_variable_matrix,
        preferred_element_type=jnp.float32,
    )
    predicted_member_states = (members_state_array.astype(jnp.float32) + increment).astype(
        jnp.bfloat16
    )[None]
    ensemble = lax.all_gather(predicted_member_states, "mem", axis=0, tiled=True)
    observed_f = observed.astype(jnp.float32)
    error_sq, pair_sq = square_sums(ensemble, observed_f)
    error_sq, pair_sq = lax.psum((error_sq, pair_sq), "space")
    errors, weights, energy_loss = loss_terms(error_sq, pair_sq, entries)
    predicted_state_derivative = members_state_derivative(
        ensemble, lax.axis_index("mem"), observed_f, errors, weights, scale_factor, entries
    )
    part_out = jnp.einsum(
        "fu,sf->us",
        inner_layer_response,
        predicted_state_derivative,
        preferred_element_type=jnp.float32,
    )
    hidden_gradient = jnp.einsum(
        "tm,lt->ml",
        predicted_state_derivative,
        decoder_variable_matrix,
        preferred_element_type=jnp.float32,
    )
    pre_grad = (hidden_gradient * silu_slope(hidden_pre)).astype(jnp.bfloat16)
    updated_grad = jnp.einsum("gk,hk->gh", pre_grad, w_hid, preferred_element_type=jnp.float32)
    edge_grad = updated_grad[:, None, :] * silu_slope(decoder_in) / dec_edges.shape[1]
    message_grad = jax.ops.segment_sum(
        edge_grad.reshape(-1, edge_grad.shape[2]),
        dec_edges.reshape(-1),
        num_segments=message.shape[0],
    ).astype(jnp.bfloat16)
    part_msg = jnp.einsum(
        "rh,rk->hk", received_mesh, message_grad, preferred_element_type=jnp.float32
    )
    grad_out, grad_msg = lax.psum((part_out, part_msg), ("space", "mem"))
    return (
        predicted_member_states,
        jnp.reshape(energy_loss, (1,)),
        grad_out,
        grad_msg.astype(jnp.bfloat16),
    )


def solution(mesh):
    in_specs = (
        P(("grp", "mem"), None, "space"),
        P("grp", "space"),
        P("space", None),
        P("space", None, None),
        P("space", None),
        P("space", None, None),
        P("space", None),
        P(),
        P(),
        P(),
        P(),
        P(),
        P(),
        P(),
        P(),
    )
    out_specs = (P(("grp", "mem"), None, "space"), P("grp"), P("grp", None), P("grp", None))
    return jax.shard_map(
        chosen, mesh=mesh, in_specs=in_specs, out_specs=out_specs, check_vma=False)
```

```python
import functools
import math

import jax
import jax.numpy as jnp
from jax import lax
from jax.experimental import pallas as pl
from jax.experimental.pallas import tpu as pltpu
from jax.sharding import PartitionSpec as P

MESH = pl.DeviceIdType.MESH
HBM = pltpu.HBM
ANY = pl.BlockSpec(memory_space=pl.ANY)
F32 = jnp.float32
BF16 = jnp.bfloat16
ROWS = 112
CHUNKS = 4


def dot(a, b, contract=(1, 0)):
    return lax.dot_general(
        a, b, (((contract[0],), (contract[1],)), ((), ())), preferred_element_type=F32
    )


def sigmoid(v):
    return 0.5 * jnp.tanh(0.5 * v) + 0.5


def silu(v):
    return v * sigmoid(v)


def slope(v):
    g = sigmoid(v)
    return g * (1.0 + v * (1.0 - g))


def one_hot(hit):
    return jnp.where(hit, 1.0, 0.0).astype(BF16)


def step_kernel(
    spaces, members,
    x_hbm, obs_hbm, feat_hbm, esend_hbm, eedge_hbm, dsend_hbm, dedge_hbm,
    w_in_hbm, w_src_hbm, w_dst_hbm, w_enc_hbm, w_msg_hbm, w_self_hbm, w_hid_hbm, dvm_t_hbm,
    pred_ref, loss_ref, gout_ref, gmsg_ref,
    x_ref, obs_ref, feat_ref, esend_ref, eedge_ref, dsend_ref, dedge_ref,
    w_in_ref, w_src_ref, w_dst_ref, w_enc_ref, w_msg_ref, w_self_ref, w_hid_ref, dvm_t_ref,
    xp, obsp, winp, dvmp, dedges,
    xs_send, xs_recv, gl, self_term, ehot, dhot, dhot_t, arr, nq,
    ms_send, ma, dec_in, hid, act, ens, st, st_recv, loss_s, loss_r, fgs,
    gos, gor, gs, gq, aall, at, q32, qb, q_recv, fin,
    in_sem, x_ss, x_rs, m_ss, m_rs, s_ss, s_rs, zq_ss, zq_rs, c1_ss, c1_rs,
    l_ss, l_rs, o_ss, o_rs, g_ss, g_rs, a_ss, a_rs, e_ss, e_rs, c2_ss, c2_rs,
):
    grp, sp, me = lax.axis_index("grp"), lax.axis_index("space"), lax.axis_index("mem")
    partner = [me, me + 1 - 2 * lax.rem(me, 2), lax.rem(me + 2, 4), 3 - me]
    varn, grid = obs_ref.shape
    latent = w_src_ref.shape[0]
    nodes = feat_ref.shape[0]
    ecap, dcap = esend_ref.shape[2], dsend_ref.shape[2]
    slots, dslots = spaces * ecap, spaces * dcap
    k_enc, k_dec = eedge_ref.shape[0], dedge_ref.shape[0]
    part = grid // CHUNKS
    entries = varn * grid * spaces
    quarter = latent // members
    zrows = latent // spaces
    orows = 128 // spaces

    loads = {}
    order = (
        (x_hbm, x_ref), (esend_hbm, esend_ref), (w_in_hbm, w_in_ref), (feat_hbm, feat_ref),
        (w_dst_hbm, w_dst_ref), (eedge_hbm, eedge_ref), (w_src_hbm, w_src_ref),
        (w_enc_hbm, w_enc_ref), (dsend_hbm, dsend_ref), (dedge_hbm, dedge_ref),
        (w_self_hbm, w_self_ref), (w_msg_hbm, w_msg_ref), (w_hid_hbm, w_hid_ref),
        (dvm_t_hbm, dvm_t_ref), (obs_hbm, obs_ref),
    )
    for i, (far, near) in enumerate(order):
        loads[id(near)] = pltpu.make_async_copy(far, near, in_sem.at[i])
        loads[id(near)].start()

    def ready(*refs):
        for ref in refs:
            loads.pop(id(ref)).wait()

    def space_at(o):
        return lax.rem(sp + o, spaces)

    def to_space(src, dst, ss, rs, o):
        copy = pltpu.make_async_remote_copy(
            src_ref=src, dst_ref=dst, send_sem=ss.at[o], recv_sem=rs.at[o],
            device_id=(grp, space_at(o), me), device_id_type=MESH,
        )
        copy.start()
        return copy

    def to_mem(src, dst, ss, rs, j):
        copy = pltpu.make_async_remote_copy(
            src_ref=src, dst_ref=dst, send_sem=ss, recv_sem=rs,
            device_id=(grp, sp, partner[j]), device_id_type=MESH,
        )
        copy.start()
        return copy

    barrier = pltpu.get_barrier_semaphore()
    for o in range(1, spaces):
        pl.semaphore_signal(barrier, inc=1, device_id=(grp, space_at(o), me), device_id_type=MESH)
    for j in range(1, members):
        pl.semaphore_signal(barrier, inc=1, device_id=(grp, sp, partner[j]), device_id_type=MESH)

    ready(x_ref, esend_ref)
    xp[96:ROWS, :] = jnp.zeros((ROWS - 96, grid), BF16)
    xp[0:varn, :] = x_ref[0]
    grid_rows = lax.broadcasted_iota(jnp.int32, (grid, ecap), 0)
    xs = {}
    for o in list(range(1, spaces)) + [0]:
        row = esend_ref[0, pl.ds(space_at(o), 1), :]
        picked = dot(xp[...], one_hot(grid_rows == row)).astype(BF16)
        if o == 0:
            xs_recv[sp] = picked
        else:
            xs_send[o] = picked
            if not xs:
                pl.semaphore_wait(barrier, spaces + members - 2)
            xs[o] = to_space(xs_send.at[o], xs_recv.at[sp], x_ss, x_rs, o)

    ready(w_in_ref, feat_ref, w_dst_ref, eedge_ref)
    winp[96:ROWS, :] = jnp.zeros((ROWS - 96, latent), BF16)
    winp[0:varn, :] = w_in_ref[...]
    nq[...] = dot(feat_ref[...], w_dst_ref[...]).astype(BF16).astype(F32)
    slot_cols = lax.broadcasted_iota(jnp.int32, (nodes, slots), 1)
    columns = eedge_ref[...].T
    for k in range(k_enc):
        ehot[k * nodes:(k + 1) * nodes, :] = one_hot(slot_cols == columns[:, k:k + 1])

    ready(w_src_ref, w_enc_ref)
    for o in range(spaces):
        if o:
            xs[o].wait()
        source = lax.rem(sp + spaces - o, spaces)
        embedded = silu(dot(xs_recv[source], winp[...], (0, 0))).astype(BF16)
        arr[source] = dot(embedded, w_src_ref[...]).astype(BF16)
    arrived = arr[...].reshape(slots, latent)
    total = jnp.zeros((nodes, latent), F32)
    group = 4
    for k in range(0, k_enc, group):
        v = dot(ehot[k * nodes:(k + group) * nodes, :], arrived)
        for i in range(group):
            total += silu(v[i * nodes:(i + 1) * nodes, :] + nq[...])
    aggregate = (total * (1.0 / k_enc)).astype(BF16)
    mesh_latent = (feat_ref[...].astype(F32) + dot(aggregate, w_enc_ref[...])).astype(BF16)

    ready(dsend_ref)
    node_rows = lax.broadcasted_iota(jnp.int32, (nodes, dcap), 0)
    ms = []
    for o in list(range(1, spaces)) + [0]:
        row = dsend_ref[0, pl.ds(space_at(o), 1), :]
        picked = dot(one_hot(node_rows == row), mesh_latent, (0, 0)).astype(BF16)
        if o == 0:
            ma[sp] = picked
        else:
            ms_send[o] = picked
            ms.append(to_space(ms_send.at[o], ma.at[sp], m_ss, m_rs, o))
    ready(dedge_ref, w_self_ref, w_msg_ref, w_hid_ref, dvm_t_ref, obs_ref)
    for c in range(CHUNKS):
        rows = slice(c * part, (c + 1) * part)
        latents = silu(dot(xp[:, rows], winp[...], (0, 0))).astype(BF16)
        gl[rows, :] = latents
        self_term[rows, :] = dot(latents, w_self_ref[...])
    dvmp[96:ROWS, :] = jnp.zeros((ROWS - 96, latent), BF16)
    dvmp[0:varn, :] = dvm_t_ref[...]
    dedges[...] = jnp.zeros((8, grid), jnp.int32)
    dedges[0:k_dec, :] = dedge_ref[...]
    dcolumns = dedges[...].T
    dcols = lax.broadcasted_iota(jnp.int32, (grid, dslots), 1)
    for k in range(k_dec):
        dhot[k] = one_hot(dcols == dcolumns[:, k:k + 1])
    for copy in ms:
        copy.wait()

    arrivals = ma[...].reshape(dslots, latent)
    aall[0] = arrivals
    message = dot(arrivals, w_msg_ref[...]).astype(BF16)
    near, far, passed = [], [], []

    def pass_on(c):
        far[c].wait()
        passed.append(to_mem(ens.at[2, c], ens.at[3, c], e_ss.at[3, c], e_rs.at[3, c], 1))

    for c in range(CHUNKS):
        rows = slice(c * part, (c + 1) * part)
        acc = jnp.zeros((part, latent), F32)
        own = self_term[rows, :]
        for k in range(k_dec):
            v = dot(dhot[k, rows, :], message) + own
            dec_in[k, rows, :] = v
            acc += silu(v)
        updated = (gl[rows, :].astype(F32) + acc * (1.0 / k_dec)).astype(BF16)
        pre = dot(updated, w_hid_ref[...])
        hid[rows, :] = pre
        response = silu(pre).astype(BF16)
        act[rows, :] = response
        increment = dot(dvmp[...], response, (1, 1))
        predicted = (xp[:, rows].astype(F32) + increment).astype(BF16)
        ens[0, c] = predicted
        far.append(to_mem(ens.at[0, c], ens.at[2, c], e_ss.at[2, c], e_rs.at[2, c], 2))
        near.append(to_mem(ens.at[0, c], ens.at[1, c], e_ss.at[1, c], e_rs.at[1, c], 1))
        pred_ref[0, :, rows] = predicted[0:varn, :]
        if c:
            pass_on(c - 1)
    a_far = to_mem(aall.at[0], aall.at[2], a_ss.at[2], a_rs.at[2], 2)
    a_near = to_mem(aall.at[0], aall.at[1], a_ss.at[1], a_rs.at[1], 1)

    obsp[96:ROWS, :] = jnp.zeros((ROWS - 96, grid), BF16)
    obsp[0:varn, :] = obs_ref[...]
    for c in range(CHUNKS):
        rows = slice(c * part, (c + 1) * part)
        hid[rows, :] = slope(hid[rows, :])
        for k in range(k_dec):
            dec_in[k, rows, :] = slope(dec_in[k, rows, :]) * (1.0 / k_dec)
        if c == 1:
            pass_on(CHUNKS - 1)

    def folded(d):
        d = (d * d).reshape(ROWS // 8, 8, part).sum(axis=0)
        out = d[:, 0:128]
        for i in range(1, part // 128):
            out += d[:, i * 128:(i + 1) * 128]
        return out

    sums = [jnp.zeros((8, 128), F32) for _ in range(members)]
    for c in range(CHUNKS):
        rows = slice(c * part, (c + 1) * part)
        near[c].wait()
        mine = ens[0, c].astype(F32)
        sums[0] += folded(mine - obsp[:, rows].astype(F32))
        sums[1] += folded(mine - ens[1, c].astype(F32))
        sums[2] += folded(mine - ens[2, c].astype(F32))
        passed[c].wait()
        sums[3] += folded(mine - ens[3, c].astype(F32))
    for j in range(members):
        st[j] = sums[j]
    ss = [to_space(st, st_recv.at[o], s_ss, s_rs, o) for o in range(1, spaces)]
    drows = lax.broadcasted_iota(jnp.int32, (dslots, grid), 0)
    for k in range(k_dec):
        dhot_t[k] = one_hot(drows == dedges[k:k + 1, :])
    a_far.wait()
    a_passed = to_mem(aall.at[2], aall.at[3], a_ss.at[3], a_rs.at[3], 1)
    for copy in ss:
        copy.wait()
    tot = st[...]
    for o in range(1, spaces):
        tot += st_recv[o]
    root = jnp.sqrt(jnp.sum(tot, axis=(1, 2), keepdims=True) / entries + 1e-06)
    error = root[0]
    my_loss = error / members
    for j in range(1, members):
        my_loss -= root[j] / (2.0 * members * members)
    loss_s[...] = jnp.broadcast_to(my_loss, (8, 128))
    scale = members * math.sqrt(entries)
    first = scale / (members * entries * error)
    pulls = [scale / (members * members * entries * root[j]) for j in range(1, members)]

    gout = jnp.zeros((ROWS, latent), F32)
    for c in range(CHUNKS):
        rows = slice(c * part, (c + 1) * part)
        mine = ens[0, c].astype(F32)
        fg = first * (mine - obsp[:, rows].astype(F32))
        for j in range(1, members):
            fg -= pulls[j - 1] * (mine - ens[j, c].astype(F32))
        fg = fg.astype(BF16)
        fgs[c] = fg
        gout += dot(fg, act[rows, :])
    for m in range(members):
        gos[m, 0:ROWS, :] = gout[:, m * quarter:(m + 1) * quarter].astype(BF16)
        gos[m, ROWS:128, :] = jnp.zeros((128 - ROWS, quarter), BF16)
    os_, ls = [], []
    for j in range(1, members):
        os_.append(to_mem(gos.at[partner[j]], gor.at[j], o_ss.at[j], o_rs.at[j], j))
        ls.append(to_mem(loss_s, loss_r.at[j], l_ss.at[j], l_rs.at[j], j))

    mgrad = jnp.zeros((dslots, latent), F32)
    for c in range(CHUNKS):
        rows = slice(c * part, (c + 1) * part)
        hgrad = dot(fgs[c], dvmp[...], (0, 0))
        pre_grad = (hgrad * hid[rows, :]).astype(BF16)
        ugrad = dot(pre_grad, w_hid_ref[...], (1, 1))
        for k in range(k_dec):
            edge = (ugrad * dec_in[k, rows, :]).astype(BF16)
            mgrad += dot(dhot_t[k, :, rows], edge)
    for m in range(members):
        gs[m] = mgrad[:, m * quarter:(m + 1) * quarter].astype(BF16)
    gsent = []
    for j in (2, 3, 1):
        gsent.append(to_mem(gs.at[partner[j]], gq.at[j], g_ss.at[j], g_rs.at[j], j))
    gq[0] = gs[me]
    a_near.wait()
    a_passed.wait()
    for j in range(members):
        at[:, j * dslots:(j + 1) * dslots] = aall[j].astype(F32).T.astype(BF16)
    for copy in os_:
        copy.wait()
    oq = gos[me].astype(F32)
    for j in range(1, members):
        oq += gor[j].astype(F32)
    oq = oq.reshape(spaces, orows, quarter)
    q32[:, zrows:, :] = oq
    qb[:, zrows:, :] = oq.astype(BF16)
    for copy in gsent:
        copy.wait()
    q = dot(at[...], gq[...].reshape(members * dslots, quarter)).reshape(spaces, zrows, quarter)
    q32[:, 0:zrows, :] = q
    qb[:, 0:zrows, :] = q.astype(BF16)
    zq = [
        to_space(qb.at[space_at(o)], q_recv.at[o], zq_ss, zq_rs, o) for o in range(1, spaces)
    ]
    r = q32[sp]
    for o in range(1, spaces):
        zq[o - 1].wait()
        r += q_recv[o].astype(F32)
    fin[0, sp] = r.astype(BF16)

    c1 = [
        to_space(fin.at[0, sp], fin.at[0, sp], c1_ss, c1_rs, o) for o in range(1, spaces)
    ]
    c_far, c_near, c_passed = [], [], []
    for o in range(spaces):
        if o:
            c1[o - 1].wait()
        at_ = lax.rem(sp + spaces - o, spaces)
        c_far.append(to_mem(fin.at[0, at_], fin.at[2, at_], c2_ss.at[2, o], c2_rs.at[2, o], 2))
        c_near.append(to_mem(fin.at[0, at_], fin.at[1, at_], c2_ss.at[1, o], c2_rs.at[1, o], 1))
    for o in range(spaces):
        at_ = lax.rem(sp + spaces - o, spaces)
        c_far[o].wait()
        c_passed.append(to_mem(fin.at[2, at_], fin.at[3, at_], c2_ss.at[3, o], c2_rs.at[3, o], 1))
    for copy in ls:
        copy.wait()
    all_loss = loss_s[...]
    for j in range(1, members):
        all_loss += loss_r[j]
    loss_ref[0] = jnp.max(all_loss)
    for copy in c_near + c_passed:
        copy.wait()
    for m in range(members):
        if m == 0:
            slot = me
        elif m == 1:
            slot = partner[1]
        elif m == 2:
            slot = partner[2]
        else:
            slot = partner[3]
        cols = slice(m * quarter, (m + 1) * quarter)
        block = fin[slot]
        gmsg_ref[:, cols] = block[:, 0:zrows, :].reshape(latent, quarter)
        gout_ref[:, cols] = block[:, zrows:, :].reshape(128, quarter)[0:varn, :].astype(F32)


def copy_kernel(a, b, c, d, a_out, b_out, c_out, d_out, sem):
    copies = [
        pltpu.make_async_copy(x, y, sem.at[i])
        for i, (x, y) in enumerate(((a, a_out), (c, c_out), (d, d_out)))
    ]
    for copy in copies:
        copy.start()
    b_out[0] = b[0]
    for copy in copies:
        copy.wait()


def fused(
    starting_states, observed, mesh_feat, enc_send, enc_edges, dec_send, dec_edges,
    w_in, w_src, w_dst, w_enc, w_msg, w_self, w_hid, decoder_variable_matrix,
):
    spaces, members = lax.axis_size("space"), lax.axis_size("mem")
    varn, grid = observed.shape
    latent = w_src.shape[0]
    nodes = mesh_feat.shape[0]
    ecap, dcap = enc_send.shape[2], dec_send.shape[2]
    slots, dslots = spaces * ecap, spaces * dcap
    k_enc, k_dec = enc_edges.shape[1], dec_edges.shape[1]
    part = grid // CHUNKS
    quarter = latent // members
    zrows = latent // spaces + 128 // spaces
    vmem = pltpu.VMEM
    operands = (
        starting_states, observed, mesh_feat, enc_send, enc_edges.T, dec_send, dec_edges.T,
        w_in, w_src, w_dst, w_enc, w_msg, w_self, w_hid, decoder_variable_matrix.T,
    )
    scratch = [vmem(operand.shape, operand.dtype) for operand in operands]
    scratch += [
        vmem((ROWS, grid), BF16), vmem((ROWS, grid), BF16),
        vmem((ROWS, latent), BF16), vmem((ROWS, latent), BF16), vmem((8, grid), jnp.int32),
        vmem((spaces, ROWS, ecap), BF16), vmem((spaces, ROWS, ecap), BF16),
        vmem((grid, latent), BF16), vmem((grid, latent), F32),
        vmem((k_enc * nodes, slots), BF16),
        vmem((k_dec, grid, dslots), BF16), vmem((k_dec, dslots, grid), BF16),
        vmem((spaces, ecap, latent), BF16), vmem((nodes, latent), F32),
        vmem((spaces, dcap, latent), BF16), vmem((spaces, dcap, latent), BF16),
        vmem((k_dec, grid, latent), F32), vmem((grid, latent), F32), vmem((grid, latent), BF16),
        vmem((members, CHUNKS, ROWS, part), BF16),
        vmem((members, 8, 128), F32), vmem((spaces, members, 8, 128), F32),
        vmem((8, 128), F32), vmem((members, 8, 128), F32),
        vmem((CHUNKS, ROWS, part), BF16),
        vmem((members, 128, quarter), BF16), vmem((members, 128, quarter), BF16),
        vmem((members, dslots, quarter), BF16), vmem((members, dslots, quarter), BF16),
        vmem((members, dslots, latent), BF16), vmem((latent, members * dslots), BF16),
        vmem((spaces, zrows, quarter), F32), vmem((spaces, zrows, quarter), BF16),
        vmem((spaces, zrows, quarter), BF16),
        vmem((members, spaces, zrows, quarter), BF16),
    ]
    dma = pltpu.SemaphoreType.DMA
    scratch += [dma((len(operands),))]
    scratch += [dma((spaces,))] * 10
    scratch += [dma((members,))] * 8
    scratch += [dma((members, CHUNKS))] * 2
    scratch += [dma((members, spaces))] * 2
    whole = pl.BlockSpec(memory_space=pltpu.VMEM)
    hbm = pl.BlockSpec(memory_space=HBM)
    smem = pl.BlockSpec(memory_space=pltpu.SMEM)
    shapes = (
        jax.ShapeDtypeStruct((1, varn, grid), BF16),
        jax.ShapeDtypeStruct((1,), F32),
        jax.ShapeDtypeStruct((varn, latent), F32),
        jax.ShapeDtypeStruct((latent, latent), BF16),
    )
    results = pl.pallas_call(
        functools.partial(step_kernel, spaces, members),
        out_shape=shapes,
        in_specs=[hbm] * len(operands),
        out_specs=(whole, smem, whole, whole),
        scratch_shapes=scratch,
        compiler_params=pltpu.CompilerParams(
            collective_id=0, has_side_effects=True, vmem_limit_bytes=64 * 1024 * 1024
        ),
    )(*operands)
    pred, loss, gout, gmsg = pl.pallas_call(
        copy_kernel,
        out_shape=shapes,
        in_specs=(ANY, smem, ANY, ANY),
        out_specs=(hbm, smem, hbm, hbm),
        scratch_shapes=[dma((3,))],
    )(*results)
    return pred, loss, gout.T, gmsg


def fits(spaces, members, latent, ecap, dcap):
    return (
        members == 4
        and latent // members == 128
        and ecap % 128 == 0
        and dcap % 16 == 0
        and latent % (16 * spaces) == 0
        and 128 % (8 * spaces) == 0
    )


def chosen(*args):
    spaces, members = lax.axis_size("space"), lax.axis_size("mem")
    if fits(spaces, members, args[8].shape[0], args[3].shape[2], args[5].shape[2]):
        return fused(*args)
    return local(*args)


def silu_slope(argument):
    logistic = jax.nn.sigmoid(argument)
    return logistic * (1.0 + argument * (1.0 - logistic))


def square_sums(row_block, observed_part):

    def per_member(member):
        member_f = member.astype(jnp.float32)
        diff = member_f - observed_part
        apart = row_block.astype(jnp.float32) - member_f[None]
        return (jnp.sum(diff * diff), jnp.sum(apart * apart, axis=(1, 2)))

    return lax.map(per_member, row_block)


def loss_terms(error_sq, pair_sq, entries):
    member_total_number = error_sq.shape[0]
    errors = jnp.sqrt(error_sq / entries + 1e-06)
    spreads = jnp.sqrt(pair_sq / entries + 1e-06)
    apart_mask = 1.0 - jnp.eye(member_total_number, dtype=jnp.float32)
    energy_loss = jnp.mean(errors) - jnp.sum(apart_mask * spreads) / (
        2.0 * member_total_number * member_total_number
    )
    weights = apart_mask / (member_total_number * member_total_number * entries * spreads)
    return (errors, weights, energy_loss)


def members_state_derivative(
    row_block, member_index, observed_part, errors, weights, scale_factor, entries
):
    member_total_number = row_block.shape[0]
    member = lax.dynamic_index_in_dim(row_block, member_index, 0, keepdims=False).astype(
        jnp.float32
    )
    first = (member - observed_part) / (member_total_number * entries * errors[member_index])

    def add_other(other_member, pulled):
        other_field = lax.dynamic_index_in_dim(row_block, other_member, 0, keepdims=False).astype(
            jnp.float32
        )
        return pulled + weights[member_index, other_member] * (member - other_field)

    pulled = lax.fori_loop(0, member_total_number, add_other, jnp.zeros_like(member))
    return (scale_factor * (first - pulled)).astype(jnp.bfloat16)


def local(
    starting_states,
    observed,
    mesh_feat,
    enc_send,
    enc_edges,
    dec_send,
    dec_edges,
    w_in,
    w_src,
    w_dst,
    w_enc,
    w_msg,
    w_self,
    w_hid,
    decoder_variable_matrix,
):
    members_state_array = starting_states[0]
    spaces = lax.axis_size("space")
    member_total_number = lax.axis_size("mem")
    entries = members_state_array.shape[0] * members_state_array.shape[1] * spaces
    scale_factor = member_total_number * math.sqrt(entries)
    grid_latent = jax.nn.silu(
        jnp.einsum("vg,vh->gh", members_state_array, w_in, preferred_element_type=jnp.float32)
    ).astype(jnp.bfloat16)
    projected = jnp.dot(grid_latent, w_src, preferred_element_type=jnp.float32).astype(jnp.bfloat16)
    outgoing = jnp.take(projected, enc_send[0], axis=0)
    arrived = lax.all_to_all(outgoing, "space", split_axis=0, concat_axis=0, tiled=True)
    received = arrived.reshape(-1, arrived.shape[2])
    node_query = jnp.dot(mesh_feat, w_dst, preferred_element_type=jnp.float32).astype(jnp.bfloat16)
    neighbours = jnp.take(received, enc_edges, axis=0).astype(jnp.float32)
    aggregate = jnp.mean(
        jax.nn.silu(neighbours + node_query.astype(jnp.float32)[:, None, :]), axis=1
    ).astype(jnp.bfloat16)
    mesh_latent = (
        mesh_feat.astype(jnp.float32)
        + jnp.dot(aggregate, w_enc, preferred_element_type=jnp.float32)
    ).astype(jnp.bfloat16)
    outgoing_mesh = jnp.take(mesh_latent, dec_send[0], axis=0)
    arrived_mesh = lax.all_to_all(outgoing_mesh, "space", split_axis=0, concat_axis=0, tiled=True)
    received_mesh = arrived_mesh.reshape(-1, arrived_mesh.shape[2])
    message = jnp.dot(received_mesh, w_msg, preferred_element_type=jnp.float32).astype(jnp.bfloat16)
    self_term = jnp.dot(grid_latent, w_self, preferred_element_type=jnp.float32)
    decoder_in = jnp.take(message, dec_edges, axis=0).astype(jnp.float32) + self_term[:, None, :]
    updated = (grid_latent.astype(jnp.float32) + jnp.mean(jax.nn.silu(decoder_in), axis=1)).astype(
        jnp.bfloat16
    )
    hidden_pre = jnp.dot(updated, w_hid, preferred_element_type=jnp.float32)
    inner_layer_response = jax.nn.silu(hidden_pre).astype(jnp.bfloat16)
    increment = jnp.einsum(
        "gh,hv->vg",
        inner_layer_response,
        decoder_variable_matrix,
        preferred_element_type=jnp.float32,
    )
    predicted_member_states = (members_state_array.astype(jnp.float32) + increment).astype(
        jnp.bfloat16
    )[None]
    ensemble = lax.all_gather(predicted_member_states, "mem", axis=0, tiled=True)
    observed_f = observed.astype(jnp.float32)
    error_sq, pair_sq = square_sums(ensemble, observed_f)
    error_sq, pair_sq = lax.psum((error_sq, pair_sq), "space")
    errors, weights, energy_loss = loss_terms(error_sq, pair_sq, entries)
    predicted_state_derivative = members_state_derivative(
        ensemble, lax.axis_index("mem"), observed_f, errors, weights, scale_factor, entries
    )
    part_out = jnp.einsum(
        "fu,sf->us",
        inner_layer_response,
        predicted_state_derivative,
        preferred_element_type=jnp.float32,
    )
    hidden_gradient = jnp.einsum(
        "tm,lt->ml",
        predicted_state_derivative,
        decoder_variable_matrix,
        preferred_element_type=jnp.float32,
    )
    pre_grad = (hidden_gradient * silu_slope(hidden_pre)).astype(jnp.bfloat16)
    updated_grad = jnp.einsum("gk,hk->gh", pre_grad, w_hid, preferred_element_type=jnp.float32)
    edge_grad = updated_grad[:, None, :] * silu_slope(decoder_in) / dec_edges.shape[1]
    message_grad = jax.ops.segment_sum(
        edge_grad.reshape(-1, edge_grad.shape[2]),
        dec_edges.reshape(-1),
        num_segments=message.shape[0],
    ).astype(jnp.bfloat16)
    part_msg = jnp.einsum(
        "rh,rk->hk", received_mesh, message_grad, preferred_element_type=jnp.float32
    )
    grad_out, grad_msg = lax.psum((part_out, part_msg), ("space", "mem"))
    return (
        predicted_member_states,
        jnp.reshape(energy_loss, (1,)),
        grad_out,
        grad_msg.astype(jnp.bfloat16),
    )


def solution(mesh):
    in_specs = (
        P(("grp", "mem"), None, "space"),
        P("grp", "space"),
        P("space", None),
        P("space", None, None),
        P("space", None),
        P("space", None, None),
        P("space", None),
        P(),
        P(),
        P(),
        P(),
        P(),
        P(),
        P(),
        P(),
    )
    out_specs = (P(("grp", "mem"), None, "space"), P("grp"), P("grp", None), P("grp", None))
    return jax.shard_map(
        chosen, mesh=mesh, in_specs=in_specs, out_specs=out_specs, check_vma=False)
```

```python
import functools
import math

import jax
import jax.numpy as jnp
from jax import lax
from jax.experimental import pallas as pl
from jax.experimental.pallas import tpu as pltpu
from jax.sharding import PartitionSpec as P

MESH = pl.DeviceIdType.MESH
HBM = pltpu.HBM
ANY = pl.BlockSpec(memory_space=pl.ANY)
F32 = jnp.float32
BF16 = jnp.bfloat16
ROWS = 112
CHUNKS = 4


def dot(a, b, contract=(1, 0)):
    return lax.dot_general(
        a, b, (((contract[0],), (contract[1],)), ((), ())), preferred_element_type=F32
    )


def sigmoid(v):
    return 0.5 * jnp.tanh(0.5 * v) + 0.5


def silu(v):
    return v * sigmoid(v)


def slope(v):
    g = sigmoid(v)
    return g * (1.0 + v * (1.0 - g))


def one_hot(hit):
    return jnp.where(hit, 1.0, 0.0).astype(BF16)


def step_kernel(
    spaces, members,
    x_hbm, obs_hbm, feat_hbm, esend_hbm, eedge_hbm, dsend_hbm, dedge_hbm,
    w_in_hbm, w_src_hbm, w_dst_hbm, w_enc_hbm, w_msg_hbm, w_self_hbm, w_hid_hbm, dvm_t_hbm,
    pred_ref, loss_ref, gout_ref, gmsg_ref,
    x_ref, obs_ref, feat_ref, esend_ref, eedge_ref, dsend_ref, dedge_ref,
    w_in_ref, w_src_ref, w_dst_ref, w_enc_ref, w_msg_ref, w_self_ref, w_hid_ref, dvm_t_ref,
    xp, obsp, winp, dvmp, dedges,
    xs_send, xs_recv, gl, self_term, ehot, dhot, dhot_t, arr, nq,
    ms_send, ma, dec_in, hid, act, ens, st, st_recv, loss_s, loss_r, fgs,
    gos, gor, gs, gq, aall, at, q32, qb, q_recv, fin,
    in_sem, x_ss, x_rs, m_ss, m_rs, s_ss, s_rs, zq_ss, zq_rs, c1_ss, c1_rs,
    l_ss, l_rs, o_ss, o_rs, g_ss, g_rs, a_ss, a_rs, e_ss, e_rs, c2_ss, c2_rs,
):
    grp, sp, me = lax.axis_index("grp"), lax.axis_index("space"), lax.axis_index("mem")
    partner = [me, me + 1 - 2 * lax.rem(me, 2), lax.rem(me + 2, 4), 3 - me]
    varn, grid = obs_ref.shape
    latent = w_src_ref.shape[0]
    nodes = feat_ref.shape[0]
    ecap, dcap = esend_ref.shape[2], dsend_ref.shape[2]
    slots, dslots = spaces * ecap, spaces * dcap
    k_enc, k_dec = eedge_ref.shape[0], dedge_ref.shape[0]
    part = grid // CHUNKS
    entries = varn * grid * spaces
    quarter = latent // members
    zrows = latent // spaces
    orows = 128 // spaces

    loads = {}
    order = (
        (x_hbm, x_ref), (esend_hbm, esend_ref), (w_in_hbm, w_in_ref), (feat_hbm, feat_ref),
        (w_dst_hbm, w_dst_ref), (eedge_hbm, eedge_ref), (w_src_hbm, w_src_ref),
        (w_enc_hbm, w_enc_ref), (dsend_hbm, dsend_ref), (dedge_hbm, dedge_ref),
        (w_self_hbm, w_self_ref), (w_msg_hbm, w_msg_ref), (w_hid_hbm, w_hid_ref),
        (dvm_t_hbm, dvm_t_ref), (obs_hbm, obs_ref),
    )
    for i, (far, near) in enumerate(order):
        loads[id(near)] = pltpu.make_async_copy(far, near, in_sem.at[i])
        loads[id(near)].start()

    def ready(*refs):
        for ref in refs:
            loads.pop(id(ref)).wait()

    def space_at(o):
        return lax.rem(sp + o, spaces)

    def to_space(src, dst, ss, rs, o):
        copy = pltpu.make_async_remote_copy(
            src_ref=src, dst_ref=dst, send_sem=ss.at[o], recv_sem=rs.at[o],
            device_id=(grp, space_at(o), me), device_id_type=MESH,
        )
        copy.start()
        return copy

    def to_mem(src, dst, ss, rs, j):
        copy = pltpu.make_async_remote_copy(
            src_ref=src, dst_ref=dst, send_sem=ss, recv_sem=rs,
            device_id=(grp, sp, partner[j]), device_id_type=MESH,
        )
        copy.start()
        return copy

    barrier = pltpu.get_barrier_semaphore()
    for o in range(1, spaces):
        pl.semaphore_signal(barrier, inc=1, device_id=(grp, space_at(o), me), device_id_type=MESH)
    for j in range(1, members):
        pl.semaphore_signal(barrier, inc=1, device_id=(grp, sp, partner[j]), device_id_type=MESH)

    ready(x_ref, esend_ref)
    xp[96:ROWS, :] = jnp.zeros((ROWS - 96, grid), BF16)
    xp[0:varn, :] = x_ref[0]
    grid_rows = lax.broadcasted_iota(jnp.int32, (grid, ecap), 0)
    xs = {}
    for o in list(range(1, spaces)) + [0]:
        row = esend_ref[0, pl.ds(space_at(o), 1), :]
        picked = dot(xp[...], one_hot(grid_rows == row)).astype(BF16)
        if o == 0:
            xs_recv[sp] = picked
        else:
            xs_send[o] = picked
            if not xs:
                pl.semaphore_wait(barrier, spaces + members - 2)
            xs[o] = to_space(xs_send.at[o], xs_recv.at[sp], x_ss, x_rs, o)

    ready(w_in_ref, feat_ref, w_dst_ref, eedge_ref)
    winp[96:ROWS, :] = jnp.zeros((ROWS - 96, latent), BF16)
    winp[0:varn, :] = w_in_ref[...]
    nq[...] = dot(feat_ref[...], w_dst_ref[...]).astype(BF16).astype(F32)
    slot_cols = lax.broadcasted_iota(jnp.int32, (nodes, slots), 1)
    columns = eedge_ref[...].T
    for k in range(k_enc):
        ehot[k * nodes:(k + 1) * nodes, :] = one_hot(slot_cols == columns[:, k:k + 1])

    ready(w_src_ref, w_enc_ref)
    for o in range(spaces):
        if o:
            xs[o].wait()
        source = lax.rem(sp + spaces - o, spaces)
        embedded = silu(dot(xs_recv[source], winp[...], (0, 0))).astype(BF16)
        arr[source] = dot(embedded, w_src_ref[...]).astype(BF16)
    arrived = arr[...].reshape(slots, latent)
    total = jnp.zeros((nodes, latent), F32)
    group = 4
    for k in range(0, k_enc, group):
        v = dot(ehot[k * nodes:(k + group) * nodes, :], arrived)
        for i in range(group):
            total += silu(v[i * nodes:(i + 1) * nodes, :] + nq[...])
    aggregate = (total * (1.0 / k_enc)).astype(BF16)
    mesh_latent = (feat_ref[...].astype(F32) + dot(aggregate, w_enc_ref[...])).astype(BF16)

    ready(dsend_ref)
    node_rows = lax.broadcasted_iota(jnp.int32, (nodes, dcap), 0)
    ms = []
    for o in list(range(1, spaces)) + [0]:
        row = dsend_ref[0, pl.ds(space_at(o), 1), :]
        picked = dot(one_hot(node_rows == row), mesh_latent, (0, 0)).astype(BF16)
        if o == 0:
            ma[sp] = picked
        else:
            ms_send[o] = picked
            ms.append(to_space(ms_send.at[o], ma.at[sp], m_ss, m_rs, o))
    ready(dedge_ref, w_self_ref, w_msg_ref, w_hid_ref, dvm_t_ref, obs_ref)
    for c in range(CHUNKS):
        rows = slice(c * part, (c + 1) * part)
        latents = silu(dot(xp[:, rows], winp[...], (0, 0))).astype(BF16)
        gl[rows, :] = latents
        self_term[rows, :] = dot(latents, w_self_ref[...])
    dvmp[96:ROWS, :] = jnp.zeros((ROWS - 96, latent), BF16)
    dvmp[0:varn, :] = dvm_t_ref[...]
    dedges[...] = jnp.zeros((8, grid), jnp.int32)
    dedges[0:k_dec, :] = dedge_ref[...]
    dcolumns = dedges[...].T
    dcols = lax.broadcasted_iota(jnp.int32, (grid, dslots), 1)
    for k in range(k_dec):
        dhot[k] = one_hot(dcols == dcolumns[:, k:k + 1])
    for copy in ms:
        copy.wait()

    arrivals = ma[...].reshape(dslots, latent)
    aall[0] = arrivals
    message = dot(arrivals, w_msg_ref[...]).astype(BF16)
    near, far, passed = [], [], []

    def pass_on(c):
        far[c].wait()
        passed.append(to_mem(ens.at[2, c], ens.at[3, c], e_ss.at[3, c], e_rs.at[3, c], 1))

    for c in range(CHUNKS):
        rows = slice(c * part, (c + 1) * part)
        acc = jnp.zeros((part, latent), F32)
        own = self_term[rows, :]
        for k in range(k_dec):
            v = dot(dhot[k, rows, :], message) + own
            dec_in[k, rows, :] = v
            acc += silu(v)
        updated = (gl[rows, :].astype(F32) + acc * (1.0 / k_dec)).astype(BF16)
        pre = dot(updated, w_hid_ref[...])
        hid[rows, :] = pre
        response = silu(pre).astype(BF16)
        act[rows, :] = response
        increment = dot(dvmp[...], response, (1, 1))
        predicted = (xp[:, rows].astype(F32) + increment).astype(BF16)
        ens[0, c] = predicted
        far.append(to_mem(ens.at[0, c], ens.at[2, c], e_ss.at[2, c], e_rs.at[2, c], 2))
        near.append(to_mem(ens.at[0, c], ens.at[1, c], e_ss.at[1, c], e_rs.at[1, c], 1))
        pred_ref[0, :, rows] = predicted[0:varn, :]
        if c:
            pass_on(c - 1)
    a_far = to_mem(aall.at[0], aall.at[2], a_ss.at[2], a_rs.at[2], 2)
    a_near = to_mem(aall.at[0], aall.at[1], a_ss.at[1], a_rs.at[1], 1)

    obsp[96:ROWS, :] = jnp.zeros((ROWS - 96, grid), BF16)
    obsp[0:varn, :] = obs_ref[...]
    for c in range(CHUNKS):
        rows = slice(c * part, (c + 1) * part)
        hid[rows, :] = slope(hid[rows, :])
        for k in range(k_dec):
            dec_in[k, rows, :] = slope(dec_in[k, rows, :]) * (1.0 / k_dec)
        if c == 1:
            pass_on(CHUNKS - 1)

    def folded(d):
        d = (d * d).reshape(ROWS // 8, 8, part).sum(axis=0)
        out = d[:, 0:128]
        for i in range(1, part // 128):
            out += d[:, i * 128:(i + 1) * 128]
        return out

    sums = [jnp.zeros((8, 128), F32) for _ in range(members)]
    for c in range(CHUNKS):
        rows = slice(c * part, (c + 1) * part)
        near[c].wait()
        mine = ens[0, c].astype(F32)
        sums[0] += folded(mine - obsp[:, rows].astype(F32))
        sums[1] += folded(mine - ens[1, c].astype(F32))
        sums[2] += folded(mine - ens[2, c].astype(F32))
        passed[c].wait()
        sums[3] += folded(mine - ens[3, c].astype(F32))
    for j in range(members):
        st[j] = sums[j]
    ss = [to_space(st, st_recv.at[o], s_ss, s_rs, o) for o in range(1, spaces)]
    drows = lax.broadcasted_iota(jnp.int32, (dslots, grid), 0)
    for k in range(k_dec):
        dhot_t[k] = one_hot(drows == dedges[k:k + 1, :])
    a_far.wait()
    a_passed = to_mem(aall.at[2], aall.at[3], a_ss.at[3], a_rs.at[3], 1)
    for copy in ss:
        copy.wait()
    tot = st[...]
    for o in range(1, spaces):
        tot += st_recv[o]
    root = jnp.sqrt(jnp.sum(tot, axis=(1, 2), keepdims=True) / entries + 1e-06)
    error = root[0]
    my_loss = error / members
    for j in range(1, members):
        my_loss -= root[j] / (2.0 * members * members)
    loss_s[...] = jnp.broadcast_to(my_loss, (8, 128))
    scale = members * math.sqrt(entries)
    first = scale / (members * entries * error)
    pulls = [scale / (members * members * entries * root[j]) for j in range(1, members)]

    gout = jnp.zeros((ROWS, latent), F32)
    for c in range(CHUNKS):
        rows = slice(c * part, (c + 1) * part)
        mine = ens[0, c].astype(F32)
        fg = first * (mine - obsp[:, rows].astype(F32))
        for j in range(1, members):
            fg -= pulls[j - 1] * (mine - ens[j, c].astype(F32))
        fg = fg.astype(BF16)
        fgs[c] = fg
        gout += dot(fg, act[rows, :])
    for m in range(members):
        gos[m, 0:ROWS, :] = gout[:, m * quarter:(m + 1) * quarter].astype(BF16)
        gos[m, ROWS:128, :] = jnp.zeros((128 - ROWS, quarter), BF16)
    os_, ls = [], []
    for j in range(1, members):
        os_.append(to_mem(gos.at[partner[j]], gor.at[j], o_ss.at[j], o_rs.at[j], j))
        ls.append(to_mem(loss_s, loss_r.at[j], l_ss.at[j], l_rs.at[j], j))

    mgrad = jnp.zeros((dslots, latent), F32)
    for c in range(CHUNKS):
        rows = slice(c * part, (c + 1) * part)
        hgrad = dot(fgs[c], dvmp[...], (0, 0))
        pre_grad = (hgrad * hid[rows, :]).astype(BF16)
        ugrad = dot(pre_grad, w_hid_ref[...], (1, 1))
        for k in range(k_dec):
            edge = (ugrad * dec_in[k, rows, :]).astype(BF16)
            mgrad += dot(dhot_t[k, :, rows], edge)
    for m in range(members):
        gs[m] = mgrad[:, m * quarter:(m + 1) * quarter].astype(BF16)
    gsent = []
    for j in (2, 3, 1):
        gsent.append(to_mem(gs.at[partner[j]], gq.at[j], g_ss.at[j], g_rs.at[j], j))
    gq[0] = gs[me]
    a_near.wait()
    a_passed.wait()
    for j in range(members):
        at[:, j * dslots:(j + 1) * dslots] = aall[j].astype(F32).T.astype(BF16)
    for copy in os_:
        copy.wait()
    oq = gos[me].astype(F32)
    for j in range(1, members):
        oq += gor[j].astype(F32)
    oq = oq.reshape(spaces, orows, quarter)
    q32[:, zrows:, :] = oq
    qb[:, zrows:, :] = oq.astype(BF16)
    for copy in gsent:
        copy.wait()
    q = dot(at[...], gq[...].reshape(members * dslots, quarter)).reshape(spaces, zrows, quarter)
    q32[:, 0:zrows, :] = q
    qb[:, 0:zrows, :] = q.astype(BF16)
    zq = [
        to_space(qb.at[space_at(o)], q_recv.at[o], zq_ss, zq_rs, o) for o in range(1, spaces)
    ]
    r = q32[sp]
    for o in range(1, spaces):
        zq[o - 1].wait()
        r += q_recv[o].astype(F32)
    fin[0, sp] = r.astype(BF16)

    c1 = [
        to_space(fin.at[0, sp], fin.at[0, sp], c1_ss, c1_rs, o) for o in range(1, spaces)
    ]
    c_far, c_near, c_passed = [], [], []
    for o in range(spaces):
        if o:
            c1[o - 1].wait()
        at_ = lax.rem(sp + spaces - o, spaces)
        c_far.append(to_mem(fin.at[0, at_], fin.at[2, at_], c2_ss.at[2, o], c2_rs.at[2, o], 2))
        c_near.append(to_mem(fin.at[0, at_], fin.at[1, at_], c2_ss.at[1, o], c2_rs.at[1, o], 1))
    for o in range(spaces):
        at_ = lax.rem(sp + spaces - o, spaces)
        c_far[o].wait()
        c_passed.append(to_mem(fin.at[2, at_], fin.at[3, at_], c2_ss.at[3, o], c2_rs.at[3, o], 1))
    for copy in ls:
        copy.wait()
    all_loss = loss_s[...]
    for j in range(1, members):
        all_loss += loss_r[j]
    loss_ref[0] = jnp.max(all_loss)
    for copy in c_near + c_passed:
        copy.wait()
    for m in range(members):
        if m == 0:
            slot = me
        elif m == 1:
            slot = partner[1]
        elif m == 2:
            slot = partner[2]
        else:
            slot = partner[3]
        cols = slice(m * quarter, (m + 1) * quarter)
        block = fin[slot]
        gmsg_ref[:, cols] = block[:, 0:zrows, :].reshape(latent, quarter)
        gout_ref[:, cols] = block[:, zrows:, :].reshape(128, quarter)[0:varn, :].astype(F32)


def copy_kernel(a, b, c, d, a_out, b_out, c_out, d_out, a_buf, c_buf, d_buf, sem):
    legs = []
    for i, (x, buf, y) in enumerate(((a, a_buf, a_out), (c, c_buf, c_out), (d, d_buf, d_out))):
        inward = pltpu.make_async_copy(x, buf, sem.at[0, i])
        inward.start()
        legs.append((inward, pltpu.make_async_copy(buf, y, sem.at[1, i])))
    b_out[0] = b[0]
    for inward, outward in legs:
        inward.wait()
        outward.start()
    for _, outward in legs:
        outward.wait()


def fused(
    starting_states, observed, mesh_feat, enc_send, enc_edges, dec_send, dec_edges,
    w_in, w_src, w_dst, w_enc, w_msg, w_self, w_hid, decoder_variable_matrix,
):
    spaces, members = lax.axis_size("space"), lax.axis_size("mem")
    varn, grid = observed.shape
    latent = w_src.shape[0]
    nodes = mesh_feat.shape[0]
    ecap, dcap = enc_send.shape[2], dec_send.shape[2]
    slots, dslots = spaces * ecap, spaces * dcap
    k_enc, k_dec = enc_edges.shape[1], dec_edges.shape[1]
    part = grid // CHUNKS
    quarter = latent // members
    zrows = latent // spaces + 128 // spaces
    vmem = pltpu.VMEM
    operands = (
        starting_states, observed, mesh_feat, enc_send, enc_edges.T, dec_send, dec_edges.T,
        w_in, w_src, w_dst, w_enc, w_msg, w_self, w_hid, decoder_variable_matrix.T,
    )
    scratch = [vmem(operand.shape, operand.dtype) for operand in operands]
    scratch += [
        vmem((ROWS, grid), BF16), vmem((ROWS, grid), BF16),
        vmem((ROWS, latent), BF16), vmem((ROWS, latent), BF16), vmem((8, grid), jnp.int32),
        vmem((spaces, ROWS, ecap), BF16), vmem((spaces, ROWS, ecap), BF16),
        vmem((grid, latent), BF16), vmem((grid, latent), F32),
        vmem((k_enc * nodes, slots), BF16),
        vmem((k_dec, grid, dslots), BF16), vmem((k_dec, dslots, grid), BF16),
        vmem((spaces, ecap, latent), BF16), vmem((nodes, latent), F32),
        vmem((spaces, dcap, latent), BF16), vmem((spaces, dcap, latent), BF16),
        vmem((k_dec, grid, latent), F32), vmem((grid, latent), F32), vmem((grid, latent), BF16),
        vmem((members, CHUNKS, ROWS, part), BF16),
        vmem((members, 8, 128), F32), vmem((spaces, members, 8, 128), F32),
        vmem((8, 128), F32), vmem((members, 8, 128), F32),
        vmem((CHUNKS, ROWS, part), BF16),
        vmem((members, 128, quarter), BF16), vmem((members, 128, quarter), BF16),
        vmem((members, dslots, quarter), BF16), vmem((members, dslots, quarter), BF16),
        vmem((members, dslots, latent), BF16), vmem((latent, members * dslots), BF16),
        vmem((spaces, zrows, quarter), F32), vmem((spaces, zrows, quarter), BF16),
        vmem((spaces, zrows, quarter), BF16),
        vmem((members, spaces, zrows, quarter), BF16),
    ]
    dma = pltpu.SemaphoreType.DMA
    scratch += [dma((len(operands),))]
    scratch += [dma((spaces,))] * 10
    scratch += [dma((members,))] * 8
    scratch += [dma((members, CHUNKS))] * 2
    scratch += [dma((members, spaces))] * 2
    whole = pl.BlockSpec(memory_space=pltpu.VMEM)
    hbm = pl.BlockSpec(memory_space=HBM)
    smem = pl.BlockSpec(memory_space=pltpu.SMEM)
    shapes = (
        jax.ShapeDtypeStruct((1, varn, grid), BF16),
        jax.ShapeDtypeStruct((1,), F32),
        jax.ShapeDtypeStruct((varn, latent), F32),
        jax.ShapeDtypeStruct((latent, latent), BF16),
    )
    results = pl.pallas_call(
        functools.partial(step_kernel, spaces, members),
        out_shape=shapes,
        in_specs=[hbm] * len(operands),
        out_specs=(whole, smem, whole, whole),
        scratch_shapes=scratch,
        compiler_params=pltpu.CompilerParams(
            collective_id=0, has_side_effects=True, vmem_limit_bytes=64 * 1024 * 1024
        ),
    )(*operands)
    pred, loss, gout, gmsg = pl.pallas_call(
        copy_kernel,
        out_shape=shapes,
        in_specs=(ANY, smem, ANY, ANY),
        out_specs=(hbm, smem, hbm, hbm),
        scratch_shapes=[
            vmem(shapes[0].shape, BF16), vmem(shapes[2].shape, F32), vmem(shapes[3].shape, BF16),
            dma((2, 3)),
        ],
        compiler_params=pltpu.CompilerParams(vmem_limit_bytes=64 * 1024 * 1024),
    )(*results)
    return pred, loss, gout.T, gmsg


def fits(spaces, members, latent, ecap, dcap):
    return (
        members == 4
        and latent // members == 128
        and ecap % 128 == 0
        and dcap % 16 == 0
        and latent % (16 * spaces) == 0
        and 128 % (8 * spaces) == 0
    )


def chosen(*args):
    spaces, members = lax.axis_size("space"), lax.axis_size("mem")
    if fits(spaces, members, args[8].shape[0], args[3].shape[2], args[5].shape[2]):
        return fused(*args)
    return local(*args)


def silu_slope(argument):
    logistic = jax.nn.sigmoid(argument)
    return logistic * (1.0 + argument * (1.0 - logistic))


def square_sums(row_block, observed_part):

    def per_member(member):
        member_f = member.astype(jnp.float32)
        diff = member_f - observed_part
        apart = row_block.astype(jnp.float32) - member_f[None]
        return (jnp.sum(diff * diff), jnp.sum(apart * apart, axis=(1, 2)))

    return lax.map(per_member, row_block)


def loss_terms(error_sq, pair_sq, entries):
    member_total_number = error_sq.shape[0]
    errors = jnp.sqrt(error_sq / entries + 1e-06)
    spreads = jnp.sqrt(pair_sq / entries + 1e-06)
    apart_mask = 1.0 - jnp.eye(member_total_number, dtype=jnp.float32)
    energy_loss = jnp.mean(errors) - jnp.sum(apart_mask * spreads) / (
        2.0 * member_total_number * member_total_number
    )
    weights = apart_mask / (member_total_number * member_total_number * entries * spreads)
    return (errors, weights, energy_loss)


def members_state_derivative(
    row_block, member_index, observed_part, errors, weights, scale_factor, entries
):
    member_total_number = row_block.shape[0]
    member = lax.dynamic_index_in_dim(row_block, member_index, 0, keepdims=False).astype(
        jnp.float32
    )
    first = (member - observed_part) / (member_total_number * entries * errors[member_index])

    def add_other(other_member, pulled):
        other_field = lax.dynamic_index_in_dim(row_block, other_member, 0, keepdims=False).astype(
            jnp.float32
        )
        return pulled + weights[member_index, other_member] * (member - other_field)

    pulled = lax.fori_loop(0, member_total_number, add_other, jnp.zeros_like(member))
    return (scale_factor * (first - pulled)).astype(jnp.bfloat16)


def local(
    starting_states,
    observed,
    mesh_feat,
    enc_send,
    enc_edges,
    dec_send,
    dec_edges,
    w_in,
    w_src,
    w_dst,
    w_enc,
    w_msg,
    w_self,
    w_hid,
    decoder_variable_matrix,
):
    members_state_array = starting_states[0]
    spaces = lax.axis_size("space")
    member_total_number = lax.axis_size("mem")
    entries = members_state_array.shape[0] * members_state_array.shape[1] * spaces
    scale_factor = member_total_number * math.sqrt(entries)
    grid_latent = jax.nn.silu(
        jnp.einsum("vg,vh->gh", members_state_array, w_in, preferred_element_type=jnp.float32)
    ).astype(jnp.bfloat16)
    projected = jnp.dot(grid_latent, w_src, preferred_element_type=jnp.float32).astype(jnp.bfloat16)
    outgoing = jnp.take(projected, enc_send[0], axis=0)
    arrived = lax.all_to_all(outgoing, "space", split_axis=0, concat_axis=0, tiled=True)
    received = arrived.reshape(-1, arrived.shape[2])
    node_query = jnp.dot(mesh_feat, w_dst, preferred_element_type=jnp.float32).astype(jnp.bfloat16)
    neighbours = jnp.take(received, enc_edges, axis=0).astype(jnp.float32)
    aggregate = jnp.mean(
        jax.nn.silu(neighbours + node_query.astype(jnp.float32)[:, None, :]), axis=1
    ).astype(jnp.bfloat16)
    mesh_latent = (
        mesh_feat.astype(jnp.float32)
        + jnp.dot(aggregate, w_enc, preferred_element_type=jnp.float32)
    ).astype(jnp.bfloat16)
    outgoing_mesh = jnp.take(mesh_latent, dec_send[0], axis=0)
    arrived_mesh = lax.all_to_all(outgoing_mesh, "space", split_axis=0, concat_axis=0, tiled=True)
    received_mesh = arrived_mesh.reshape(-1, arrived_mesh.shape[2])
    message = jnp.dot(received_mesh, w_msg, preferred_element_type=jnp.float32).astype(jnp.bfloat16)
    self_term = jnp.dot(grid_latent, w_self, preferred_element_type=jnp.float32)
    decoder_in = jnp.take(message, dec_edges, axis=0).astype(jnp.float32) + self_term[:, None, :]
    updated = (grid_latent.astype(jnp.float32) + jnp.mean(jax.nn.silu(decoder_in), axis=1)).astype(
        jnp.bfloat16
    )
    hidden_pre = jnp.dot(updated, w_hid, preferred_element_type=jnp.float32)
    inner_layer_response = jax.nn.silu(hidden_pre).astype(jnp.bfloat16)
    increment = jnp.einsum(
        "gh,hv->vg",
        inner_layer_response,
        decoder_variable_matrix,
        preferred_element_type=jnp.float32,
    )
    predicted_member_states = (members_state_array.astype(jnp.float32) + increment).astype(
        jnp.bfloat16
    )[None]
    ensemble = lax.all_gather(predicted_member_states, "mem", axis=0, tiled=True)
    observed_f = observed.astype(jnp.float32)
    error_sq, pair_sq = square_sums(ensemble, observed_f)
    error_sq, pair_sq = lax.psum((error_sq, pair_sq), "space")
    errors, weights, energy_loss = loss_terms(error_sq, pair_sq, entries)
    predicted_state_derivative = members_state_derivative(
        ensemble, lax.axis_index("mem"), observed_f, errors, weights, scale_factor, entries
    )
    part_out = jnp.einsum(
        "fu,sf->us",
        inner_layer_response,
        predicted_state_derivative,
        preferred_element_type=jnp.float32,
    )
    hidden_gradient = jnp.einsum(
        "tm,lt->ml",
        predicted_state_derivative,
        decoder_variable_matrix,
        preferred_element_type=jnp.float32,
    )
    pre_grad = (hidden_gradient * silu_slope(hidden_pre)).astype(jnp.bfloat16)
    updated_grad = jnp.einsum("gk,hk->gh", pre_grad, w_hid, preferred_element_type=jnp.float32)
    edge_grad = updated_grad[:, None, :] * silu_slope(decoder_in) / dec_edges.shape[1]
    message_grad = jax.ops.segment_sum(
        edge_grad.reshape(-1, edge_grad.shape[2]),
        dec_edges.reshape(-1),
        num_segments=message.shape[0],
    ).astype(jnp.bfloat16)
    part_msg = jnp.einsum(
        "rh,rk->hk", received_mesh, message_grad, preferred_element_type=jnp.float32
    )
    grad_out, grad_msg = lax.psum((part_out, part_msg), ("space", "mem"))
    return (
        predicted_member_states,
        jnp.reshape(energy_loss, (1,)),
        grad_out,
        grad_msg.astype(jnp.bfloat16),
    )


def solution(mesh):
    in_specs = (
        P(("grp", "mem"), None, "space"),
        P("grp", "space"),
        P("space", None),
        P("space", None, None),
        P("space", None),
        P("space", None, None),
        P("space", None),
        P(),
        P(),
        P(),
        P(),
        P(),
        P(),
        P(),
        P(),
    )
    out_specs = (P(("grp", "mem"), None, "space"), P("grp"), P("grp", None), P("grp", None))
    return jax.shard_map(
        chosen, mesh=mesh, in_specs=in_specs, out_specs=out_specs, check_vma=False)
```

```python
import functools
import math

import jax
import jax.numpy as jnp
from jax import lax
from jax.experimental import pallas as pl
from jax.experimental.pallas import tpu as pltpu
from jax.sharding import PartitionSpec as P

MESH = pl.DeviceIdType.MESH
HBM = pltpu.HBM
ANY = pl.BlockSpec(memory_space=pl.ANY)
F32 = jnp.float32
BF16 = jnp.bfloat16
ROWS = 112
CHUNKS = 4


def dot(a, b, contract=(1, 0)):
    return lax.dot_general(
        a, b, (((contract[0],), (contract[1],)), ((), ())), preferred_element_type=F32
    )


def sigmoid(v):
    return 0.5 * jnp.tanh(0.5 * v) + 0.5


def silu(v):
    return v * sigmoid(v)


def slope(v):
    g = sigmoid(v)
    return g * (1.0 + v * (1.0 - g))


def one_hot(hit):
    return jnp.where(hit, 1.0, 0.0).astype(BF16)


def step_kernel(
    spaces, members,
    x_hbm, obs_hbm, feat_hbm, esend_hbm, eedge_hbm, dsend_hbm, dedge_hbm,
    w_in_hbm, w_src_hbm, w_dst_hbm, w_enc_hbm, w_msg_hbm, w_self_hbm, w_hid_hbm, dvm_t_hbm,
    pred_ref, loss_ref, gout_ref, gmsg_ref,
    x_ref, obs_ref, feat_ref, esend_ref, eedge_ref, dsend_ref, dedge_ref,
    w_in_ref, w_src_ref, w_dst_ref, w_enc_ref, w_msg_ref, w_self_ref, w_hid_ref, dvm_t_ref,
    xp, obsp, winp, dvmp, dedges,
    xs_send, xs_recv, gl, self_term, ehot, dhot, dhot_t, arr, nq,
    ms_send, ma, dec_in, hid, act, ens, st, st_recv, loss_s, loss_r, fgs,
    gos, gor, gs, gq, aall, at, q32, qb, q_recv, fin,
    in_sem, x_ss, x_rs, m_ss, m_rs, s_ss, s_rs, zq_ss, zq_rs, c1_ss, c1_rs,
    l_ss, l_rs, o_ss, o_rs, g_ss, g_rs, a_ss, a_rs, e_ss, e_rs, c2_ss, c2_rs,
):
    grp, sp, me = lax.axis_index("grp"), lax.axis_index("space"), lax.axis_index("mem")
    partner = [me, me + 1 - 2 * lax.rem(me, 2), lax.rem(me + 2, 4), 3 - me]
    varn, grid = obs_ref.shape
    latent = w_src_ref.shape[0]
    nodes = feat_ref.shape[0]
    ecap, dcap = esend_ref.shape[2], dsend_ref.shape[2]
    slots, dslots = spaces * ecap, spaces * dcap
    k_enc, k_dec = eedge_ref.shape[0], dedge_ref.shape[0]
    part = grid // CHUNKS
    entries = varn * grid * spaces
    quarter = latent // members
    zrows = latent // spaces
    orows = 128 // spaces

    loads = {}
    order = (
        (x_hbm, x_ref), (esend_hbm, esend_ref), (w_in_hbm, w_in_ref), (feat_hbm, feat_ref),
        (w_dst_hbm, w_dst_ref), (eedge_hbm, eedge_ref), (w_src_hbm, w_src_ref),
        (w_enc_hbm, w_enc_ref), (dsend_hbm, dsend_ref), (dedge_hbm, dedge_ref),
        (w_self_hbm, w_self_ref), (w_msg_hbm, w_msg_ref), (w_hid_hbm, w_hid_ref),
        (dvm_t_hbm, dvm_t_ref), (obs_hbm, obs_ref),
    )
    for i, (far, near) in enumerate(order):
        loads[id(near)] = pltpu.make_async_copy(far, near, in_sem.at[i])
        loads[id(near)].start()

    def ready(*refs):
        for ref in refs:
            loads.pop(id(ref)).wait()

    def space_at(o):
        return lax.rem(sp + o, spaces)

    def to_space(src, dst, ss, rs, o):
        copy = pltpu.make_async_remote_copy(
            src_ref=src, dst_ref=dst, send_sem=ss.at[o], recv_sem=rs.at[o],
            device_id=(grp, space_at(o), me), device_id_type=MESH,
        )
        copy.start()
        return copy

    def to_mem(src, dst, ss, rs, j):
        copy = pltpu.make_async_remote_copy(
            src_ref=src, dst_ref=dst, send_sem=ss, recv_sem=rs,
            device_id=(grp, sp, partner[j]), device_id_type=MESH,
        )
        copy.start()
        return copy

    barrier = pltpu.get_barrier_semaphore()
    for o in range(1, spaces):
        pl.semaphore_signal(barrier, inc=1, device_id=(grp, space_at(o), me), device_id_type=MESH)
    for j in range(1, members):
        pl.semaphore_signal(barrier, inc=1, device_id=(grp, sp, partner[j]), device_id_type=MESH)

    ready(x_ref, esend_ref)
    xp[96:ROWS, :] = jnp.zeros((ROWS - 96, grid), BF16)
    xp[0:varn, :] = x_ref[0]
    grid_rows = lax.broadcasted_iota(jnp.int32, (grid, ecap), 0)
    xs = {}
    for o in list(range(1, spaces)) + [0]:
        row = esend_ref[0, pl.ds(space_at(o), 1), :]
        picked = dot(xp[...], one_hot(grid_rows == row)).astype(BF16)
        if o == 0:
            xs_recv[sp] = picked
        else:
            xs_send[o] = picked
            if not xs:
                pl.semaphore_wait(barrier, spaces + members - 2)
            xs[o] = to_space(xs_send.at[o], xs_recv.at[sp], x_ss, x_rs, o)

    ready(w_in_ref, feat_ref, w_dst_ref, eedge_ref)
    winp[96:ROWS, :] = jnp.zeros((ROWS - 96, latent), BF16)
    winp[0:varn, :] = w_in_ref[...]
    nq[...] = dot(feat_ref[...], w_dst_ref[...]).astype(BF16).astype(F32)
    slot_cols = lax.broadcasted_iota(jnp.int32, (nodes, slots), 1)
    columns = eedge_ref[...].T
    for k in range(k_enc):
        ehot[k * nodes:(k + 1) * nodes, :] = one_hot(slot_cols == columns[:, k:k + 1])

    ready(w_src_ref, w_enc_ref)
    for o in range(spaces):
        if o:
            xs[o].wait()
        source = lax.rem(sp + spaces - o, spaces)
        embedded = silu(dot(xs_recv[source], winp[...], (0, 0))).astype(BF16)
        arr[source] = dot(embedded, w_src_ref[...]).astype(BF16)
    arrived = arr[...].reshape(slots, latent)
    total = jnp.zeros((nodes, latent), F32)
    group = 4
    for k in range(0, k_enc, group):
        v = dot(ehot[k * nodes:(k + group) * nodes, :], arrived)
        for i in range(group):
            total += silu(v[i * nodes:(i + 1) * nodes, :] + nq[...])
    aggregate = (total * (1.0 / k_enc)).astype(BF16)
    mesh_latent = (feat_ref[...].astype(F32) + dot(aggregate, w_enc_ref[...])).astype(BF16)

    ready(dsend_ref)
    node_rows = lax.broadcasted_iota(jnp.int32, (nodes, dcap), 0)
    ms = []
    for o in list(range(1, spaces)) + [0]:
        row = dsend_ref[0, pl.ds(space_at(o), 1), :]
        picked = dot(one_hot(node_rows == row), mesh_latent, (0, 0)).astype(BF16)
        if o == 0:
            ma[sp] = picked
        else:
            ms_send[o] = picked
            ms.append(to_space(ms_send.at[o], ma.at[sp], m_ss, m_rs, o))
    ready(dedge_ref, w_self_ref, w_msg_ref, w_hid_ref, dvm_t_ref, obs_ref)
    for c in range(CHUNKS):
        rows = slice(c * part, (c + 1) * part)
        latents = silu(dot(xp[:, rows], winp[...], (0, 0))).astype(BF16)
        gl[rows, :] = latents
        self_term[rows, :] = dot(latents, w_self_ref[...])
    dvmp[96:ROWS, :] = jnp.zeros((ROWS - 96, latent), BF16)
    dvmp[0:varn, :] = dvm_t_ref[...]
    dedges[...] = jnp.zeros((8, grid), jnp.int32)
    dedges[0:k_dec, :] = dedge_ref[...]
    dcolumns = dedges[...].T
    dcols = lax.broadcasted_iota(jnp.int32, (grid, dslots), 1)
    for k in range(k_dec):
        dhot[k] = one_hot(dcols == dcolumns[:, k:k + 1])
    for copy in ms:
        copy.wait()

    arrivals = ma[...].reshape(dslots, latent)
    aall[0] = arrivals
    message = dot(arrivals, w_msg_ref[...]).astype(BF16)
    near, far, passed = [], [], []

    def pass_on(c):
        far[c].wait()
        passed.append(to_mem(ens.at[2, c], ens.at[3, c], e_ss.at[3, c], e_rs.at[3, c], 1))

    for c in range(CHUNKS):
        rows = slice(c * part, (c + 1) * part)
        acc = jnp.zeros((part, latent), F32)
        own = self_term[rows, :]
        for k in range(k_dec):
            v = dot(dhot[k, rows, :], message) + own
            dec_in[k, rows, :] = v
            acc += silu(v)
        updated = (gl[rows, :].astype(F32) + acc * (1.0 / k_dec)).astype(BF16)
        pre = dot(updated, w_hid_ref[...])
        hid[rows, :] = pre
        response = silu(pre).astype(BF16)
        act[rows, :] = response
        increment = dot(dvmp[...], response, (1, 1))
        predicted = (xp[:, rows].astype(F32) + increment).astype(BF16)
        ens[0, c] = predicted
        far.append(to_mem(ens.at[0, c], ens.at[2, c], e_ss.at[2, c], e_rs.at[2, c], 2))
        near.append(to_mem(ens.at[0, c], ens.at[1, c], e_ss.at[1, c], e_rs.at[1, c], 1))
        pred_ref[0, :, rows] = predicted[0:varn, :]
        if c:
            pass_on(c - 1)
    a_far = to_mem(aall.at[0], aall.at[2], a_ss.at[2], a_rs.at[2], 2)
    a_near = to_mem(aall.at[0], aall.at[1], a_ss.at[1], a_rs.at[1], 1)

    obsp[96:ROWS, :] = jnp.zeros((ROWS - 96, grid), BF16)
    obsp[0:varn, :] = obs_ref[...]
    for c in range(CHUNKS):
        rows = slice(c * part, (c + 1) * part)
        hid[rows, :] = slope(hid[rows, :])
        for k in range(k_dec):
            dec_in[k, rows, :] = slope(dec_in[k, rows, :]) * (1.0 / k_dec)
        if c == 1:
            pass_on(CHUNKS - 1)

    def folded(d):
        d = (d * d).reshape(ROWS // 8, 8, part).sum(axis=0)
        out = d[:, 0:128]
        for i in range(1, part // 128):
            out += d[:, i * 128:(i + 1) * 128]
        return out

    sums = [jnp.zeros((8, 128), F32) for _ in range(members)]
    for c in range(CHUNKS):
        rows = slice(c * part, (c + 1) * part)
        near[c].wait()
        mine = ens[0, c].astype(F32)
        sums[0] += folded(mine - obsp[:, rows].astype(F32))
        sums[1] += folded(mine - ens[1, c].astype(F32))
        sums[2] += folded(mine - ens[2, c].astype(F32))
        passed[c].wait()
        sums[3] += folded(mine - ens[3, c].astype(F32))
    for j in range(members):
        st[j] = sums[j]
    ss = [to_space(st, st_recv.at[o], s_ss, s_rs, o) for o in range(1, spaces)]
    drows = lax.broadcasted_iota(jnp.int32, (dslots, grid), 0)
    for k in range(k_dec):
        dhot_t[k] = one_hot(drows == dedges[k:k + 1, :])
    for copy in ss:
        copy.wait()
    tot = st[...]
    for o in range(1, spaces):
        tot += st_recv[o]
    root = jnp.sqrt(jnp.sum(tot, axis=(1, 2), keepdims=True) / entries + 1e-06)
    error = root[0]
    my_loss = error / members
    for j in range(1, members):
        my_loss -= root[j] / (2.0 * members * members)
    loss_s[...] = jnp.broadcast_to(my_loss, (8, 128))
    scale = members * math.sqrt(entries)
    first = scale / (members * entries * error)
    pulls = [scale / (members * members * entries * root[j]) for j in range(1, members)]

    gout = jnp.zeros((ROWS, latent), F32)
    for c in range(CHUNKS):
        rows = slice(c * part, (c + 1) * part)
        mine = ens[0, c].astype(F32)
        fg = first * (mine - obsp[:, rows].astype(F32))
        for j in range(1, members):
            fg -= pulls[j - 1] * (mine - ens[j, c].astype(F32))
        fg = fg.astype(BF16)
        fgs[c] = fg
        gout += dot(fg, act[rows, :])
    for m in range(members):
        gos[m, 0:ROWS, :] = gout[:, m * quarter:(m + 1) * quarter].astype(BF16)
        gos[m, ROWS:128, :] = jnp.zeros((128 - ROWS, quarter), BF16)
    os_, ls = [], []
    for j in range(1, members):
        os_.append(to_mem(gos.at[partner[j]], gor.at[j], o_ss.at[j], o_rs.at[j], j))
        ls.append(to_mem(loss_s, loss_r.at[j], l_ss.at[j], l_rs.at[j], j))

    a_far.wait()
    a_passed = to_mem(aall.at[2], aall.at[3], a_ss.at[3], a_rs.at[3], 1)

    mgrad = jnp.zeros((dslots, latent), F32)
    for c in range(CHUNKS):
        rows = slice(c * part, (c + 1) * part)
        hgrad = dot(fgs[c], dvmp[...], (0, 0))
        pre_grad = (hgrad * hid[rows, :]).astype(BF16)
        ugrad = dot(pre_grad, w_hid_ref[...], (1, 1))
        for k in range(k_dec):
            edge = (ugrad * dec_in[k, rows, :]).astype(BF16)
            mgrad += dot(dhot_t[k, :, rows], edge)
    for m in range(members):
        gs[m] = mgrad[:, m * quarter:(m + 1) * quarter].astype(BF16)
    gsent = []
    for j in (2, 3, 1):
        gsent.append(to_mem(gs.at[partner[j]], gq.at[j], g_ss.at[j], g_rs.at[j], j))
    gq[0] = gs[me]
    a_near.wait()
    a_passed.wait()
    for j in range(members):
        at[:, j * dslots:(j + 1) * dslots] = aall[j].astype(F32).T.astype(BF16)
    for copy in os_:
        copy.wait()
    oq = gos[me].astype(F32)
    for j in range(1, members):
        oq += gor[j].astype(F32)
    oq = oq.reshape(spaces, orows, quarter)
    q32[:, zrows:, :] = oq
    qb[:, zrows:, :] = oq.astype(BF16)
    for copy in gsent:
        copy.wait()
    q = dot(at[...], gq[...].reshape(members * dslots, quarter)).reshape(spaces, zrows, quarter)
    q32[:, 0:zrows, :] = q
    qb[:, 0:zrows, :] = q.astype(BF16)
    zq = [
        to_space(qb.at[space_at(o)], q_recv.at[o], zq_ss, zq_rs, o) for o in range(1, spaces)
    ]
    r = q32[sp]
    for o in range(1, spaces):
        zq[o - 1].wait()
        r += q_recv[o].astype(F32)
    fin[0, sp] = r.astype(BF16)

    c1 = [
        to_space(fin.at[0, sp], fin.at[0, sp], c1_ss, c1_rs, o) for o in range(1, spaces)
    ]
    c_far, c_near, c_passed = [], [], []
    for o in range(spaces):
        if o:
            c1[o - 1].wait()
        at_ = lax.rem(sp + spaces - o, spaces)
        c_far.append(to_mem(fin.at[0, at_], fin.at[2, at_], c2_ss.at[2, o], c2_rs.at[2, o], 2))
        c_near.append(to_mem(fin.at[0, at_], fin.at[1, at_], c2_ss.at[1, o], c2_rs.at[1, o], 1))
    for o in range(spaces):
        at_ = lax.rem(sp + spaces - o, spaces)
        c_far[o].wait()
        c_passed.append(to_mem(fin.at[2, at_], fin.at[3, at_], c2_ss.at[3, o], c2_rs.at[3, o], 1))
    for copy in ls:
        copy.wait()
    all_loss = loss_s[...]
    for j in range(1, members):
        all_loss += loss_r[j]
    loss_ref[0] = jnp.max(all_loss)
    for copy in c_near + c_passed:
        copy.wait()
    for m in range(members):
        if m == 0:
            slot = me
        elif m == 1:
            slot = partner[1]
        elif m == 2:
            slot = partner[2]
        else:
            slot = partner[3]
        cols = slice(m * quarter, (m + 1) * quarter)
        block = fin[slot]
        gmsg_ref[:, cols] = block[:, 0:zrows, :].reshape(latent, quarter)
        gout_ref[:, cols] = block[:, zrows:, :].reshape(128, quarter)[0:varn, :].astype(F32)


def copy_kernel(a, b, c, d, a_out, b_out, c_out, d_out, a_buf, c_buf, d_buf, sem):
    legs = []
    for i, (x, buf, y) in enumerate(((a, a_buf, a_out), (c, c_buf, c_out), (d, d_buf, d_out))):
        inward = pltpu.make_async_copy(x, buf, sem.at[0, i])
        inward.start()
        legs.append((inward, pltpu.make_async_copy(buf, y, sem.at[1, i])))
    b_out[0] = b[0]
    for inward, outward in legs:
        inward.wait()
        outward.start()
    for _, outward in legs:
        outward.wait()


def fused(
    starting_states, observed, mesh_feat, enc_send, enc_edges, dec_send, dec_edges,
    w_in, w_src, w_dst, w_enc, w_msg, w_self, w_hid, decoder_variable_matrix,
):
    spaces, members = lax.axis_size("space"), lax.axis_size("mem")
    varn, grid = observed.shape
    latent = w_src.shape[0]
    nodes = mesh_feat.shape[0]
    ecap, dcap = enc_send.shape[2], dec_send.shape[2]
    slots, dslots = spaces * ecap, spaces * dcap
    k_enc, k_dec = enc_edges.shape[1], dec_edges.shape[1]
    part = grid // CHUNKS
    quarter = latent // members
    zrows = latent // spaces + 128 // spaces
    vmem = pltpu.VMEM
    operands = (
        starting_states, observed, mesh_feat, enc_send, enc_edges.T, dec_send, dec_edges.T,
        w_in, w_src, w_dst, w_enc, w_msg, w_self, w_hid, decoder_variable_matrix.T,
    )
    scratch = [vmem(operand.shape, operand.dtype) for operand in operands]
    scratch += [
        vmem((ROWS, grid), BF16), vmem((ROWS, grid), BF16),
        vmem((ROWS, latent), BF16), vmem((ROWS, latent), BF16), vmem((8, grid), jnp.int32),
        vmem((spaces, ROWS, ecap), BF16), vmem((spaces, ROWS, ecap), BF16),
        vmem((grid, latent), BF16), vmem((grid, latent), F32),
        vmem((k_enc * nodes, slots), BF16),
        vmem((k_dec, grid, dslots), BF16), vmem((k_dec, dslots, grid), BF16),
        vmem((spaces, ecap, latent), BF16), vmem((nodes, latent), F32),
        vmem((spaces, dcap, latent), BF16), vmem((spaces, dcap, latent), BF16),
        vmem((k_dec, grid, latent), F32), vmem((grid, latent), F32), vmem((grid, latent), BF16),
        vmem((members, CHUNKS, ROWS, part), BF16),
        vmem((members, 8, 128), F32), vmem((spaces, members, 8, 128), F32),
        vmem((8, 128), F32), vmem((members, 8, 128), F32),
        vmem((CHUNKS, ROWS, part), BF16),
        vmem((members, 128, quarter), BF16), vmem((members, 128, quarter), BF16),
        vmem((members, dslots, quarter), BF16), vmem((members, dslots, quarter), BF16),
        vmem((members, dslots, latent), BF16), vmem((latent, members * dslots), BF16),
        vmem((spaces, zrows, quarter), F32), vmem((spaces, zrows, quarter), BF16),
        vmem((spaces, zrows, quarter), BF16),
        vmem((members, spaces, zrows, quarter), BF16),
    ]
    dma = pltpu.SemaphoreType.DMA
    scratch += [dma((len(operands),))]
    scratch += [dma((spaces,))] * 10
    scratch += [dma((members,))] * 8
    scratch += [dma((members, CHUNKS))] * 2
    scratch += [dma((members, spaces))] * 2
    whole = pl.BlockSpec(memory_space=pltpu.VMEM)
    hbm = pl.BlockSpec(memory_space=HBM)
    smem = pl.BlockSpec(memory_space=pltpu.SMEM)
    shapes = (
        jax.ShapeDtypeStruct((1, varn, grid), BF16),
        jax.ShapeDtypeStruct((1,), F32),
        jax.ShapeDtypeStruct((varn, latent), F32),
        jax.ShapeDtypeStruct((latent, latent), BF16),
    )
    results = pl.pallas_call(
        functools.partial(step_kernel, spaces, members),
        out_shape=shapes,
        in_specs=[hbm] * len(operands),
        out_specs=(whole, smem, whole, whole),
        scratch_shapes=scratch,
        compiler_params=pltpu.CompilerParams(
            collective_id=0, has_side_effects=True, vmem_limit_bytes=64 * 1024 * 1024
        ),
    )(*operands)
    pred, loss, gout, gmsg = pl.pallas_call(
        copy_kernel,
        out_shape=shapes,
        in_specs=(ANY, smem, ANY, ANY),
        out_specs=(hbm, smem, hbm, hbm),
        scratch_shapes=[
            vmem(shapes[0].shape, BF16), vmem(shapes[2].shape, F32), vmem(shapes[3].shape, BF16),
            dma((2, 3)),
        ],
        compiler_params=pltpu.CompilerParams(vmem_limit_bytes=64 * 1024 * 1024),
    )(*results)
    return pred, loss, gout.T, gmsg


def fits(spaces, members, latent, ecap, dcap):
    return (
        members == 4
        and latent // members == 128
        and ecap % 128 == 0
        and dcap % 16 == 0
        and latent % (16 * spaces) == 0
        and 128 % (8 * spaces) == 0
    )


def chosen(*args):
    spaces, members = lax.axis_size("space"), lax.axis_size("mem")
    if fits(spaces, members, args[8].shape[0], args[3].shape[2], args[5].shape[2]):
        return fused(*args)
    return local(*args)


def silu_slope(argument):
    logistic = jax.nn.sigmoid(argument)
    return logistic * (1.0 + argument * (1.0 - logistic))


def square_sums(row_block, observed_part):

    def per_member(member):
        member_f = member.astype(jnp.float32)
        diff = member_f - observed_part
        apart = row_block.astype(jnp.float32) - member_f[None]
        return (jnp.sum(diff * diff), jnp.sum(apart * apart, axis=(1, 2)))

    return lax.map(per_member, row_block)


def loss_terms(error_sq, pair_sq, entries):
    member_total_number = error_sq.shape[0]
    errors = jnp.sqrt(error_sq / entries + 1e-06)
    spreads = jnp.sqrt(pair_sq / entries + 1e-06)
    apart_mask = 1.0 - jnp.eye(member_total_number, dtype=jnp.float32)
    energy_loss = jnp.mean(errors) - jnp.sum(apart_mask * spreads) / (
        2.0 * member_total_number * member_total_number
    )
    weights = apart_mask / (member_total_number * member_total_number * entries * spreads)
    return (errors, weights, energy_loss)


def members_state_derivative(
    row_block, member_index, observed_part, errors, weights, scale_factor, entries
):
    member_total_number = row_block.shape[0]
    member = lax.dynamic_index_in_dim(row_block, member_index, 0, keepdims=False).astype(
        jnp.float32
    )
    first = (member - observed_part) / (member_total_number * entries * errors[member_index])

    def add_other(other_member, pulled):
        other_field = lax.dynamic_index_in_dim(row_block, other_member, 0, keepdims=False).astype(
            jnp.float32
        )
        return pulled + weights[member_index, other_member] * (member - other_field)

    pulled = lax.fori_loop(0, member_total_number, add_other, jnp.zeros_like(member))
    return (scale_factor * (first - pulled)).astype(jnp.bfloat16)


def local(
    starting_states,
    observed,
    mesh_feat,
    enc_send,
    enc_edges,
    dec_send,
    dec_edges,
    w_in,
    w_src,
    w_dst,
    w_enc,
    w_msg,
    w_self,
    w_hid,
    decoder_variable_matrix,
):
    members_state_array = starting_states[0]
    spaces = lax.axis_size("space")
    member_total_number = lax.axis_size("mem")
    entries = members_state_array.shape[0] * members_state_array.shape[1] * spaces
    scale_factor = member_total_number * math.sqrt(entries)
    grid_latent = jax.nn.silu(
        jnp.einsum("vg,vh->gh", members_state_array, w_in, preferred_element_type=jnp.float32)
    ).astype(jnp.bfloat16)
    projected = jnp.dot(grid_latent, w_src, preferred_element_type=jnp.float32).astype(jnp.bfloat16)
    outgoing = jnp.take(projected, enc_send[0], axis=0)
    arrived = lax.all_to_all(outgoing, "space", split_axis=0, concat_axis=0, tiled=True)
    received = arrived.reshape(-1, arrived.shape[2])
    node_query = jnp.dot(mesh_feat, w_dst, preferred_element_type=jnp.float32).astype(jnp.bfloat16)
    neighbours = jnp.take(received, enc_edges, axis=0).astype(jnp.float32)
    aggregate = jnp.mean(
        jax.nn.silu(neighbours + node_query.astype(jnp.float32)[:, None, :]), axis=1
    ).astype(jnp.bfloat16)
    mesh_latent = (
        mesh_feat.astype(jnp.float32)
        + jnp.dot(aggregate, w_enc, preferred_element_type=jnp.float32)
    ).astype(jnp.bfloat16)
    outgoing_mesh = jnp.take(mesh_latent, dec_send[0], axis=0)
    arrived_mesh = lax.all_to_all(outgoing_mesh, "space", split_axis=0, concat_axis=0, tiled=True)
    received_mesh = arrived_mesh.reshape(-1, arrived_mesh.shape[2])
    message = jnp.dot(received_mesh, w_msg, preferred_element_type=jnp.float32).astype(jnp.bfloat16)
    self_term = jnp.dot(grid_latent, w_self, preferred_element_type=jnp.float32)
    decoder_in = jnp.take(message, dec_edges, axis=0).astype(jnp.float32) + self_term[:, None, :]
    updated = (grid_latent.astype(jnp.float32) + jnp.mean(jax.nn.silu(decoder_in), axis=1)).astype(
        jnp.bfloat16
    )
    hidden_pre = jnp.dot(updated, w_hid, preferred_element_type=jnp.float32)
    inner_layer_response = jax.nn.silu(hidden_pre).astype(jnp.bfloat16)
    increment = jnp.einsum(
        "gh,hv->vg",
        inner_layer_response,
        decoder_variable_matrix,
        preferred_element_type=jnp.float32,
    )
    predicted_member_states = (members_state_array.astype(jnp.float32) + increment).astype(
        jnp.bfloat16
    )[None]
    ensemble = lax.all_gather(predicted_member_states, "mem", axis=0, tiled=True)
    observed_f = observed.astype(jnp.float32)
    error_sq, pair_sq = square_sums(ensemble, observed_f)
    error_sq, pair_sq = lax.psum((error_sq, pair_sq), "space")
    errors, weights, energy_loss = loss_terms(error_sq, pair_sq, entries)
    predicted_state_derivative = members_state_derivative(
        ensemble, lax.axis_index("mem"), observed_f, errors, weights, scale_factor, entries
    )
    part_out = jnp.einsum(
        "fu,sf->us",
        inner_layer_response,
        predicted_state_derivative,
        preferred_element_type=jnp.float32,
    )
    hidden_gradient = jnp.einsum(
        "tm,lt->ml",
        predicted_state_derivative,
        decoder_variable_matrix,
        preferred_element_type=jnp.float32,
    )
    pre_grad = (hidden_gradient * silu_slope(hidden_pre)).astype(jnp.bfloat16)
    updated_grad = jnp.einsum("gk,hk->gh", pre_grad, w_hid, preferred_element_type=jnp.float32)
    edge_grad = updated_grad[:, None, :] * silu_slope(decoder_in) / dec_edges.shape[1]
    message_grad = jax.ops.segment_sum(
        edge_grad.reshape(-1, edge_grad.shape[2]),
        dec_edges.reshape(-1),
        num_segments=message.shape[0],
    ).astype(jnp.bfloat16)
    part_msg = jnp.einsum(
        "rh,rk->hk", received_mesh, message_grad, preferred_element_type=jnp.float32
    )
    grad_out, grad_msg = lax.psum((part_out, part_msg), ("space", "mem"))
    return (
        predicted_member_states,
        jnp.reshape(energy_loss, (1,)),
        grad_out,
        grad_msg.astype(jnp.bfloat16),
    )


def solution(mesh):
    in_specs = (
        P(("grp", "mem"), None, "space"),
        P("grp", "space"),
        P("space", None),
        P("space", None, None),
        P("space", None),
        P("space", None, None),
        P("space", None),
        P(),
        P(),
        P(),
        P(),
        P(),
        P(),
        P(),
        P(),
    )
    out_specs = (P(("grp", "mem"), None, "space"), P("grp"), P("grp", None), P("grp", None))
    return jax.shard_map(
        chosen, mesh=mesh, in_specs=in_specs, out_specs=out_specs, check_vma=False)
```
